32 devices in a mesh: seq: 8 (over y, x, core), chan: 4 (over z).
Axes of the slice: x: 2, y: 2, z: 4, core: 2. Of those that a mesh axis runs over, the one named last changes fastest.
Arguments:
- q_in: bfloat16 [1024, 4096], P('seq', 'chan'), may hold values from -6 to 6
- k_in: bfloat16 [1024, 4096], P('seq', 'chan'), may hold values from -6 to 6
- v_in: bfloat16 [1024, 4096], P('seq', 'chan'), may hold values from -6 to 6
- short_filters: float32 [3, 3, 4096], P(None, None, 'chan'), may hold values from -3.5 to 3.5
- long_filter: float32 [4, 1024, 1024], P('chan', 'seq'), may hold values from -8 to 8
- out_weight: bfloat16 [4096, 4096], P('chan'), may hold values from -0.09375 to 0.09375
- out_grad: bfloat16 [1024, 4096], P('seq', 'chan'), may hold values from -0.059814453 to 0.059814453
Outputs:
- operator_out: bfloat16 [1024, 4096], P('seq', 'chan')
- filter_grad: float32 [4, 1024, 1024], P('chan', 'seq')
The draws below stay inside these ranges and needn't reach their ends.
All inputs are finite; a program needn't handle non-finite values.
Results may differ from the reference program's by a relative error of at most 0.0058.
Values may be sent and summed in bfloat16 or wider, within the bound.
A program may use at most 64 MiB of HBM per device.

```python
import math
import jax
import jax.numpy as jnp
from jax import lax

D = 4096
TAPS = 3
LEN = 1024
GROUPS = 4
GROUP_W = 1024


def draw_long_filter(key, part):
    rate_key, noise_key = jax.random.split(jax.random.fold_in(key, 17))
    shape = (GROUPS, GROUP_W, LEN)
    rate = jnp.exp(jax.random.uniform(rate_key, (GROUPS, GROUP_W, 1), jnp.float32, math.log(0.5), math.log(600.0)))
    noise = jnp.clip(jax.random.normal(noise_key, shape, jnp.float32), -4.0, 4.0)
    place = jnp.arange(LEN, dtype=jnp.float32)[None, None, :] / LEN
    amplitude = jnp.sqrt(2.0 * rate / LEN)
    return jnp.clip(amplitude * jnp.exp(-rate * place) * noise, -8.0, 8.0).astype(jnp.float32)


def level_of(stream_key, dims, cuts, smallest, high):
    def one(axis_at, shards_of):
        heights = jax.random.uniform(jax.random.fold_in(jax.random.fold_in(stream_key, 6), axis_at), (shards_of,), jnp.float32, smallest / len(cuts), high / len(cuts))
        return jnp.repeat(jnp.exp(heights), dims[axis_at] // shards_of).reshape((-1,) + (1,) * (len(dims) - axis_at - 1))

    gain = one(*cuts[0])
    for cut in cuts[1:]:
        gain = gain * one(*cut)
    return gain


def gaussian(key, extent, deviation, bound, cuts=(), kind=jnp.bfloat16):
    loudness = level_of(key, extent, cuts, -0.22, 0.18) if cuts else 1.0
    array = jax.random.normal(key, extent, jnp.float32) * deviation * loudness
    return jnp.minimum(jnp.maximum(array, -bound), bound).astype(kind)


def setup_inputs(seed: int = 0) -> dict:
    splits = jax.random.split(jax.random.key(seed), 8)
    return {
        "q_in": gaussian(splits[0], (LEN, D), 1.0, 6.0, ((0, 8), (1, 4))),
        "k_in": gaussian(splits[1], (LEN, D), 1.0, 6.0, ((0, 8), (1, 4))),
        "v_in": gaussian(splits[2], (LEN, D), 1.0, 6.0, ((0, 8), (1, 4))),
        "short_filters": gaussian(splits[3], (3, TAPS, D), TAPS ** -0.5, 3.5, ((2, 4),), jnp.float32),
        "long_filter": draw_long_filter(jax.random.fold_in(splits[7], 71), 0),
        "out_weight": gaussian(splits[5], (D, D), D ** -0.5, 0.09375, ((0, 4),)),
        "out_grad": gaussian(splits[6], (LEN, D), 0.01, 0.059814453, ((0, 8), (1, 4))),
    }


def short_conv(stream, taps):
    count = taps.shape[0]
    length = stream.shape[0]
    padded = jnp.concatenate((jnp.zeros((count - 1, stream.shape[1]), jnp.float32), stream), axis=0)
    result = jnp.zeros_like(stream)
    for lag in range(count):
        result = result + taps[lag][None, :] * padded[count - 1 - lag:count - 1 - lag + length]
    return result


def reference(q_in, k_in, v_in, short_filters, long_filter, out_weight, out_grad):
    q_conv = short_conv(q_in.astype(jnp.float32), short_filters[0])
    k_conv = short_conv(k_in.astype(jnp.float32), short_filters[1])
    v_conv = short_conv(v_in.astype(jnp.float32), short_filters[2])
    gated = lax.optimization_barrier((k_conv * v_conv).astype(jnp.bfloat16))
    grad_gate = jnp.dot(out_grad, out_weight.T, preferred_element_type=jnp.float32)
    dy_gate = lax.optimization_barrier((grad_gate * q_conv).astype(jnp.bfloat16))
    total = 2 * LEN
    z_groups = gated.astype(jnp.float32).T.reshape(GROUPS, GROUP_W, LEN)
    d_groups = dy_gate.astype(jnp.float32).T.reshape(GROUPS, GROUP_W, LEN)

    def one_group(items):
        z_part, h_part, d_part = items
        z_spec = jnp.fft.rfft(z_part, n=total, axis=1)
        h_spec = jnp.fft.rfft(h_part, n=total, axis=1)
        d_spec = jnp.fft.rfft(d_part, n=total, axis=1)
        y_part = jnp.fft.irfft(z_spec * h_spec, n=total, axis=1)[:, :LEN].astype(jnp.bfloat16)
        h_grad = jnp.fft.irfft(jnp.conj(z_spec) * d_spec, n=total, axis=1)[:, :LEN].astype(jnp.float32)
        return y_part, h_grad

    y_groups, filter_grad = lax.map(one_group, (z_groups, long_filter, d_groups))
    y_long = lax.optimization_barrier(y_groups.reshape(D, LEN).T)
    operator_out = (q_conv * y_long.astype(jnp.float32)).astype(jnp.bfloat16)
    return operator_out, filter_grad
```

```python
import functools
import math

import jax
import jax.numpy as jnp
from jax import lax
from jax.experimental import pallas as pl
from jax.experimental.pallas import tpu as pltpu
from jax.sharding import PartitionSpec as P

HIGHEST = lax.Precision.HIGHEST


def shifted(value, axis, steps):
    count = lax.axis_size(axis)
    leading, last = (max(0, -steps), min(count, count - steps))
    return lax.ppermute(value, axis, [(source, source + steps) for source in range(leading, last)])


def angle_table(rows, cols, modulus):
    first = jnp.arange(rows, dtype=jnp.int32)[:, None]
    second = jnp.arange(cols, dtype=jnp.int32)[None, :]
    phase = (first * second % modulus).astype(jnp.float32) * (2.0 * math.pi / modulus)
    return (jnp.cos(phase), jnp.sin(phase))


def spectrum(signal, rows_p, cols_q):
    cos_p, sin_p = angle_table(rows_p // 2, rows_p, rows_p)
    first_re = jnp.einsum("cnq,nk->ckq", signal, cos_p, precision=HIGHEST)
    first_im = -jnp.einsum("cnq,nk->ckq", signal, sin_p, precision=HIGHEST)
    cos_t, sin_t = angle_table(rows_p, cols_q, rows_p * cols_q)
    turn_re = first_re * cos_t + first_im * sin_t
    turn_im = first_im * cos_t - first_re * sin_t
    cos_q, sin_q = angle_table(cols_q, cols_q, cols_q)
    out_re = jnp.einsum("ckq,qm->ckm", turn_re, cos_q, precision=HIGHEST) + jnp.einsum(
        "ckq,qm->ckm", turn_im, sin_q, precision=HIGHEST
    )
    out_im = jnp.einsum("ckq,qm->ckm", turn_im, cos_q, precision=HIGHEST) - jnp.einsum(
        "ckq,qm->ckm", turn_re, sin_q, precision=HIGHEST
    )
    return (out_re, out_im)


def signal_back(spec_re, spec_im, rows_p, cols_q):
    cos_q, sin_q = angle_table(cols_q, cols_q, cols_q)
    mid_re = jnp.einsum("ckm,mq->ckq", spec_re, cos_q, precision=HIGHEST) - jnp.einsum(
        "ckm,mq->ckq", spec_im, sin_q, precision=HIGHEST
    )
    mid_im = jnp.einsum("ckm,mq->ckq", spec_re, sin_q, precision=HIGHEST) + jnp.einsum(
        "ckm,mq->ckq", spec_im, cos_q, precision=HIGHEST
    )
    cos_t, sin_t = angle_table(rows_p, cols_q, rows_p * cols_q)
    turn_re = mid_re * cos_t - mid_im * sin_t
    turn_im = mid_re * sin_t + mid_im * cos_t
    cos_p, sin_p = angle_table(rows_p, rows_p // 2, rows_p)
    real_part = jnp.einsum("ckq,kn->cnq", turn_re, cos_p, precision=HIGHEST) - jnp.einsum(
        "ckq,kn->cnq", turn_im, sin_p, precision=HIGHEST
    )
    return real_part / (rows_p * cols_q)


def regroup(blocked):
    return lax.all_to_all(blocked, "seq", split_axis=0, concat_axis=1, tiled=True)


def on_device_by_spectrum(q_in, k_in, v_in, short_filters, long_filter, out_weight, out_grad):
    tokens, group_w = q_in.shape
    taps = short_filters.shape[1]
    streams = jnp.stack((q_in, k_in, v_in))
    before = shifted(streams[:, tokens - (taps - 1) :, :], "seq", 1)
    extended = jnp.concatenate((before, streams), axis=1).astype(jnp.float32)
    conv = short_filters[:, 0, None, :] * extended[:, taps - 1 : taps - 1 + tokens, :]
    for lag in range(1, taps):
        conv = (
            conv
            + short_filters[:, lag, None, :]
            * extended[:, taps - 1 - lag : taps - 1 - lag + tokens, :]
        )
    q_conv = conv[0]
    gated_t = (conv[1] * conv[2]).astype(jnp.bfloat16).T
    channels = long_filter.shape[1]
    length = long_filter.shape[2]
    cols_q = length // tokens
    rows_p = 2 * tokens
    filters = long_filter.reshape(channels, tokens, cols_q)
    z_chan = regroup(gated_t)
    z_re, z_im = spectrum(
        z_chan.astype(jnp.float32).reshape(channels, tokens, cols_q), rows_p, cols_q
    )
    h_re, h_im = spectrum(filters, rows_p, cols_q)
    y_chan = signal_back(z_re * h_re - z_im * h_im, z_re * h_im + z_im * h_re, rows_p, cols_q)
    y_chan = y_chan.reshape(channels, length).astype(jnp.bfloat16)
    y_tok = lax.all_to_all(y_chan, "seq", split_axis=1, concat_axis=0, tiled=True)
    operator_out = (q_conv * y_tok.T.astype(jnp.float32)).astype(jnp.bfloat16)
    grad_gate = jnp.einsum(
        "tw,iw->ti",
        lax.all_gather(out_grad, "chan", axis=1, tiled=True),
        out_weight,
        preferred_element_type=jnp.float32,
    )
    dy_chan = regroup((grad_gate * q_conv).astype(jnp.bfloat16).T)
    d_re, d_im = spectrum(
        dy_chan.astype(jnp.float32).reshape(channels, tokens, cols_q), rows_p, cols_q
    )
    filter_grad = signal_back(z_re * d_re + z_im * d_im, z_re * d_im - z_im * d_re, rows_p, cols_q)
    return (operator_out, filter_grad.reshape(1, channels, length))


MESH = pl.DeviceIdType.MESH
BLOCK = 128
CHUNKS = 4
F32 = jnp.float32
BF16 = jnp.bfloat16


def rows_at(start, size):
    return pl.ds(pl.multiple_of(start, size), size)


def kernel(
    q_hbm, k_hbm, v_hbm, taps_hbm, filt_hbm, weight_hbm, grad_hbm,
    out_ref, fgrad_ref,
    streams, halo, taps, filt, weight, grads,
    q_t, g_send, g_recv, g_wide, toep, h_pad, y_tiles, y_send, y_recv,
    acc, d_send, d_recv, d_pad, f_tiles,
    load_sem, halo_ssem, halo_rsem, gather_ssem, gather_rsem, fwd_ssem,
    g_ssem, g_rsem, y_ssem, y_rsem, d_ssem, d_rsem,
):
    n = g_recv.shape[0]
    me, c = lax.axis_index("seq"), lax.axis_index("chan")
    streams_hbm = (q_hbm, k_hbm, v_hbm)
    cols = grads.shape[2] // CHUNKS

    loads = [pltpu.make_async_copy(ref, streams.at[s], load_sem.at[s]) for s, ref in enumerate(streams_hbm)]
    loads.append(pltpu.make_async_copy(taps_hbm, taps, load_sem.at[3]))
    own_grad = pltpu.make_async_copy(grad_hbm, grads.at[c], load_sem.at[4])
    weight_load = pltpu.make_async_copy(weight_hbm, weight, load_sem.at[5])
    filt_loads = [
        pltpu.make_async_copy(filt_hbm.at[0, :, pl.ds(a * BLOCK, BLOCK)], filt.at[a], load_sem.at[6 + a])
        for a in range(n)
    ]
    for copy in (*loads, own_grad, *filt_loads, weight_load):
        copy.start()

    barrier = pltpu.get_barrier_semaphore()
    for r in range(1, n):
        pl.semaphore_signal(barrier, inc=1, device_id=(lax.rem(me + r, n), c), device_id_type=MESH)
    for r in range(1, 4):
        pl.semaphore_signal(barrier, inc=1, device_id=(me, lax.rem(c + r, 4)), device_id_type=MESH)
    pl.semaphore_wait(barrier, n - 1 + 3)

    nxt = lax.rem(me + 1, n)
    halo_copies = [
        pltpu.make_async_remote_copy(
            src_ref=ref.at[pl.ds(BLOCK - 16, 16), :], dst_ref=halo.at[s],
            send_sem=halo_ssem.at[s], recv_sem=halo_rsem.at[s],
            device_id=(nxt, c), device_id_type=MESH,
        )
        for s, ref in enumerate(streams_hbm)
    ]

    @pl.when(me < n - 1)
    def _():
        for copy in halo_copies:
            copy.start()

    @pl.when(me == 0)
    def _():
        halo[...] = jnp.zeros_like(halo)

    partner = c + 1 - 2 * lax.rem(c, 2)
    half = c // 2
    near = 2 - half
    far = 3 - 3 * half
    middle = jnp.logical_or(c == 1, c == 2)

    def gather_copy(block, chunk, src, dst_chan, ssem):
        return pltpu.make_async_remote_copy(
            src_ref=src, dst_ref=grads.at[block, :, pl.ds(chunk * cols, cols)],
            send_sem=ssem, recv_sem=gather_rsem.at[block, chunk],
            device_id=(me, dst_chan), device_id_type=MESH,
        )

    own_sends = []
    for chunk in range(CHUNKS):
        src = grad_hbm.at[:, pl.ds(chunk * cols, cols)]
        own_sends.append(gather_copy(c, chunk, src, partner, gather_ssem.at[0, chunk]))
        own_sends.append(gather_copy(c, chunk, src, near, gather_ssem.at[1, chunk]))
    for copy in own_sends:
        copy.start()

    def forward_copy(which, block, chunk):
        src = grads.at[block, :, pl.ds(chunk * cols, cols)]
        return gather_copy(block, chunk, src, partner, fwd_ssem.at[which, chunk])

    def forward(chunk):
        @pl.when(middle)
        def _():
            for which, block in enumerate((near, far)):
                copy = forward_copy(which, block, chunk)
                copy.wait_recv()
                copy.start()

    for copy in loads:
        copy.wait()

    @pl.when(me > 0)
    def _():
        for copy in halo_copies:
            copy.wait_recv()

    row = lax.broadcasted_iota(jnp.int32, (BLOCK, BLOCK), 0)
    lane = lax.broadcasted_iota(jnp.int32, (BLOCK, BLOCK), 1)
    flip = jnp.where(row + lane == BLOCK - 1, 1.0, 0.0).astype(BF16)

    def exchange(send_ref, recv_ref, ssem, rsem, r):
        return pltpu.make_async_remote_copy(
            src_ref=send_ref.at[lax.rem(me + r, n)], dst_ref=recv_ref.at[me],
            send_sem=ssem.at[r], recv_sem=rsem.at[r],
            device_id=(lax.rem(me + r, n), c), device_id_type=MESH,
        )

    @pl.loop(1, n + 1)
    def _(r):
        p = lax.rem(me + r, n)
        here = rows_at(p * BLOCK, BLOCK)
        conv = []
        for s in range(3):
            value = streams[s, :, here].astype(F32)
            tail = halo[s, :, here].astype(F32)
            total = taps[s, 0:1, here] * value
            one = jnp.where(row == 0, tail[15:16, :], pltpu.roll(value, 1, 0))
            total = total + taps[s, 1:2, here] * one
            two = pltpu.roll(value, 2, 0)
            two = jnp.where(row == 0, tail[14:15, :], jnp.where(row == 1, tail[15:16, :], two))
            conv.append(total + taps[s, 2:3, here] * two)
        q_t[here, :] = conv[0].T
        gated = (conv[1] * conv[2]).astype(BF16).astype(F32)
        turned = jnp.dot(gated.T.astype(BF16), flip, preferred_element_type=F32)
        g_send[p] = turned.astype(BF16)

        @pl.when(r < n)
        def _():
            exchange(g_send, g_recv, g_ssem, g_rsem, r).start()

        @pl.when(r == n)
        def _():
            g_recv[me] = turned.astype(BF16)

    h_pad[...] = jnp.zeros_like(h_pad)
    d_pad[...] = jnp.zeros_like(d_pad)
    for a in range(n):
        filt_loads[a].wait()
        value = filt[a]
        high = value.astype(BF16)
        low = (value - high.astype(F32)).astype(BF16)
        turned = jnp.dot(high, flip, preferred_element_type=F32) + jnp.dot(low, flip, preferred_element_type=F32)
        h_pad[pl.ds(n + a, BLOCK, stride=2 * n), :] = turned

    forward(0)
    for r in range(1, n):
        exchange(g_send, g_recv, g_ssem, g_rsem, r).wait_recv()
    g_wide[...] = g_recv[...].astype(F32)

    def channel(d):
        rolled = None
        for u in range(n):
            before = rolled
            source = jnp.broadcast_to(g_wide[u, pl.ds(d, 1), :], (BLOCK, BLOCK))
            rolled = pltpu.roll(source, 1, 1, stride=1, stride_axis=0)
            other = jnp.zeros_like(rolled) if before is None else before
            toep[d, u * BLOCK : (u + 1) * BLOCK, :] = jnp.where(lane <= row, rolled, other).astype(BF16)
        left = jnp.concatenate([h_pad[pl.ds(d * 2 * n + n - u, n), :] for u in range(n)], axis=1)
        high = left.astype(BF16).astype(F32)
        both = jnp.concatenate([high, left - high], axis=0).astype(BF16)
        result = jnp.dot(both, toep[d], preferred_element_type=F32)
        y_tiles[rows_at(d * n, n), :] = result[:n] + result[n:]

    def channels(first, last):
        @pl.loop(first // 2, last // 2)
        def _(pair):
            channel(pair * 2)
            channel(pair * 2 + 1)

    forward(1)
    channels(0, 32)
    forward(2)
    channels(32, 64)
    forward(3)
    channels(64, BLOCK)

    for u in range(n):
        y_send[u] = y_tiles[pl.ds(u, BLOCK, stride=n), :].astype(BF16)
    for r in range(1, n):
        exchange(y_send, y_recv, y_ssem, y_rsem, r).start()
    y_recv[me] = y_send[me]

    weight_load.wait()
    own_grad.wait()
    for at, block in enumerate((c, partner, near, far)):
        if at:
            @pl.when(jnp.logical_or(jnp.logical_not(middle), at == 1))
            def _():
                for chunk in range(CHUNKS):
                    gather_copy(block, chunk, grad_hbm.at[:, pl.ds(chunk * cols, cols)], partner, gather_ssem.at[0, chunk]).wait_recv()

        wide = grads.shape[2]

        @pl.loop(0, 4)
        def _(part):
            size = acc.shape[0] // 4
            here = rows_at(part * size, size)
            term = lax.dot_general(
                weight[here, rows_at(block * wide, wide)], grads[block],
                (((1,), (1,)), ((), ())), preferred_element_type=F32,
            )
            acc[here, :] = term if at == 0 else acc[here, :] + term

    for r in range(1, n + 1):
        p = lax.rem(me + r, n)
        here = rows_at(p * BLOCK, BLOCK)
        value = (acc[here, :] * q_t[here, :]).astype(BF16)
        if r < n:
            d_send[p] = value
            exchange(d_send, d_recv, d_ssem, d_rsem, r).start()
        else:
            d_recv[me] = value

    for r in range(1, n):
        exchange(y_send, y_recv, y_ssem, y_rsem, r).wait_recv()

    @pl.loop(0, n)
    def _(p):
        here = rows_at(p * BLOCK, BLOCK)
        y = jnp.dot(y_recv[p], flip, preferred_element_type=F32)
        out_ref[:, here] = (q_t[here, :] * y).T.astype(BF16)

    for r in range(1, n):
        exchange(d_send, d_recv, d_ssem, d_rsem, r).wait_recv()
    for u in range(n):
        d_pad[pl.ds(u, BLOCK, stride=2 * n), :] = d_recv[u].astype(F32)

    @pl.loop(0, BLOCK // 4)
    def _(four):
        for i in range(4):
            d = four * 4 + i
            left = jnp.concatenate([d_pad[pl.ds(d * 2 * n + u, n), :] for u in range(n)], axis=1)
            f_tiles[rows_at(d * n, n), :] = jnp.dot(left.astype(BF16), toep[d], preferred_element_type=F32)

    for s in range(n):
        fgrad_ref[0, :, s * BLOCK : (s + 1) * BLOCK] = f_tiles[pl.ds(s, BLOCK, stride=n), :]

    @pl.when(me < n - 1)
    def _():
        for copy in halo_copies:
            copy.wait_send()

    for copy in own_sends:
        copy.wait_send()

    @pl.when(middle)
    def _():
        for chunk in range(CHUNKS):
            for which, block in enumerate((near, far)):
                forward_copy(which, block, chunk).wait_send()

    for r in range(1, n):
        exchange(g_send, g_recv, g_ssem, g_rsem, r).wait_send()
        exchange(y_send, y_recv, y_ssem, y_rsem, r).wait_send()
        exchange(d_send, d_recv, d_ssem, d_rsem, r).wait_send()


def on_device(q_in, k_in, v_in, short_filters, long_filter, out_weight, out_grad):
    tokens, group_w = q_in.shape
    taps = short_filters.shape[1]
    channels, length = long_filter.shape[1:]
    n, chans = lax.axis_size("seq"), lax.axis_size("chan")
    fits = (tokens, channels, n, chans, taps, length) == (BLOCK, BLOCK, 8, 4, 3, 8 * BLOCK)
    if not fits or out_weight.shape != (n * BLOCK, chans * group_w):
        return on_device_by_spectrum(q_in, k_in, v_in, short_filters, long_filter, out_weight, out_grad)
    dma = pltpu.SemaphoreType.DMA
    blocks = (n, BLOCK, BLOCK)
    return pl.pallas_call(
        kernel,
        out_shape=(
            jax.ShapeDtypeStruct(q_in.shape, BF16),
            jax.ShapeDtypeStruct(long_filter.shape, F32),
        ),
        in_specs=[pl.BlockSpec(memory_space=pl.ANY)] * 7,
        out_specs=[pl.BlockSpec(memory_space=pltpu.VMEM)] * 2,
        scratch_shapes=[
            pltpu.VMEM((3, tokens, group_w), BF16),
            pltpu.VMEM((3, 16, group_w), BF16),
            pltpu.VMEM(short_filters.shape, F32),
            pltpu.VMEM(blocks, F32),
            pltpu.VMEM(out_weight.shape, BF16),
            pltpu.VMEM((chans, tokens, group_w), BF16),
            pltpu.VMEM((group_w, tokens), F32),
            pltpu.VMEM(blocks, BF16),
            pltpu.VMEM(blocks, BF16),
            pltpu.VMEM(blocks, F32),
            pltpu.VMEM((channels, length, BLOCK), BF16),
            pltpu.VMEM((channels * 2 * n, BLOCK), F32),
            pltpu.VMEM((channels * n, BLOCK), F32),
            pltpu.VMEM(blocks, BF16),
            pltpu.VMEM(blocks, BF16),
            pltpu.VMEM((group_w, tokens), F32),
            pltpu.VMEM(blocks, BF16),
            pltpu.VMEM(blocks, BF16),
            pltpu.VMEM((channels * 2 * n, BLOCK), F32),
            pltpu.VMEM((channels * n, BLOCK), F32),
            dma((6 + n,)),
            dma((3,)),
            dma((3,)),
            dma((2, CHUNKS)),
            dma((chans, CHUNKS)),
            dma((2, CHUNKS)),
            dma((n,)),
            dma((n,)),
            dma((n,)),
            dma((n,)),
            dma((n,)),
            dma((n,)),
        ],
        compiler_params=pltpu.CompilerParams(
            collective_id=0, has_side_effects=True, vmem_limit_bytes=60 * 1024 * 1024
        ),
    )(q_in, k_in, v_in, short_filters, long_filter, out_weight, out_grad)


def solution(mesh):
    in_specs = (
        P("seq", "chan"),
        P("seq", "chan"),
        P("seq", "chan"),
        P(None, None, "chan"),
        P("chan", "seq", None),
        P("chan", None),
        P("seq", "chan"),
    )
    out_specs = (P("seq", "chan"), P("chan", "seq", None))
    return jax.shard_map(
        on_device, mesh=mesh, in_specs=in_specs, out_specs=out_specs, check_vma=False
    )
```

```python
import functools
import math

import jax
import jax.numpy as jnp
from jax import lax
from jax.experimental import pallas as pl
from jax.experimental.pallas import tpu as pltpu
from jax.sharding import PartitionSpec as P

HIGHEST = lax.Precision.HIGHEST


def shifted(value, axis, steps):
    count = lax.axis_size(axis)
    leading, last = (max(0, -steps), min(count, count - steps))
    return lax.ppermute(value, axis, [(source, source + steps) for source in range(leading, last)])


def angle_table(rows, cols, modulus):
    first = jnp.arange(rows, dtype=jnp.int32)[:, None]
    second = jnp.arange(cols, dtype=jnp.int32)[None, :]
    phase = (first * second % modulus).astype(jnp.float32) * (2.0 * math.pi / modulus)
    return (jnp.cos(phase), jnp.sin(phase))


def spectrum(signal, rows_p, cols_q):
    cos_p, sin_p = angle_table(rows_p // 2, rows_p, rows_p)
    first_re = jnp.einsum("cnq,nk->ckq", signal, cos_p, precision=HIGHEST)
    first_im = -jnp.einsum("cnq,nk->ckq", signal, sin_p, precision=HIGHEST)
    cos_t, sin_t = angle_table(rows_p, cols_q, rows_p * cols_q)
    turn_re = first_re * cos_t + first_im * sin_t
    turn_im = first_im * cos_t - first_re * sin_t
    cos_q, sin_q = angle_table(cols_q, cols_q, cols_q)
    out_re = jnp.einsum("ckq,qm->ckm", turn_re, cos_q, precision=HIGHEST) + jnp.einsum(
        "ckq,qm->ckm", turn_im, sin_q, precision=HIGHEST
    )
    out_im = jnp.einsum("ckq,qm->ckm", turn_im, cos_q, precision=HIGHEST) - jnp.einsum(
        "ckq,qm->ckm", turn_re, sin_q, precision=HIGHEST
    )
    return (out_re, out_im)


def signal_back(spec_re, spec_im, rows_p, cols_q):
    cos_q, sin_q = angle_table(cols_q, cols_q, cols_q)
    mid_re = jnp.einsum("ckm,mq->ckq", spec_re, cos_q, precision=HIGHEST) - jnp.einsum(
        "ckm,mq->ckq", spec_im, sin_q, precision=HIGHEST
    )
    mid_im = jnp.einsum("ckm,mq->ckq", spec_re, sin_q, precision=HIGHEST) + jnp.einsum(
        "ckm,mq->ckq", spec_im, cos_q, precision=HIGHEST
    )
    cos_t, sin_t = angle_table(rows_p, cols_q, rows_p * cols_q)
    turn_re = mid_re * cos_t - mid_im * sin_t
    turn_im = mid_re * sin_t + mid_im * cos_t
    cos_p, sin_p = angle_table(rows_p, rows_p // 2, rows_p)
    real_part = jnp.einsum("ckq,kn->cnq", turn_re, cos_p, precision=HIGHEST) - jnp.einsum(
        "ckq,kn->cnq", turn_im, sin_p, precision=HIGHEST
    )
    return real_part / (rows_p * cols_q)


def regroup(blocked):
    return lax.all_to_all(blocked, "seq", split_axis=0, concat_axis=1, tiled=True)


def on_device_by_spectrum(q_in, k_in, v_in, short_filters, long_filter, out_weight, out_grad):
    tokens, group_w = q_in.shape
    taps = short_filters.shape[1]
    streams = jnp.stack((q_in, k_in, v_in))
    before = shifted(streams[:, tokens - (taps - 1) :, :], "seq", 1)
    extended = jnp.concatenate((before, streams), axis=1).astype(jnp.float32)
    conv = short_filters[:, 0, None, :] * extended[:, taps - 1 : taps - 1 + tokens, :]
    for lag in range(1, taps):
        conv = (
            conv
            + short_filters[:, lag, None, :]
            * extended[:, taps - 1 - lag : taps - 1 - lag + tokens, :]
        )
    q_conv = conv[0]
    gated_t = (conv[1] * conv[2]).astype(jnp.bfloat16).T
    channels = long_filter.shape[1]
    length = long_filter.shape[2]
    cols_q = length // tokens
    rows_p = 2 * tokens
    filters = long_filter.reshape(channels, tokens, cols_q)
    z_chan = regroup(gated_t)
    z_re, z_im = spectrum(
        z_chan.astype(jnp.float32).reshape(channels, tokens, cols_q), rows_p, cols_q
    )
    h_re, h_im = spectrum(filters, rows_p, cols_q)
    y_chan = signal_back(z_re * h_re - z_im * h_im, z_re * h_im + z_im * h_re, rows_p, cols_q)
    y_chan = y_chan.reshape(channels, length).astype(jnp.bfloat16)
    y_tok = lax.all_to_all(y_chan, "seq", split_axis=1, concat_axis=0, tiled=True)
    operator_out = (q_conv * y_tok.T.astype(jnp.float32)).astype(jnp.bfloat16)
    grad_gate = jnp.einsum(
        "tw,iw->ti",
        lax.all_gather(out_grad, "chan", axis=1, tiled=True),
        out_weight,
        preferred_element_type=jnp.float32,
    )
    dy_chan = regroup((grad_gate * q_conv).astype(jnp.bfloat16).T)
    d_re, d_im = spectrum(
        dy_chan.astype(jnp.float32).reshape(channels, tokens, cols_q), rows_p, cols_q
    )
    filter_grad = signal_back(z_re * d_re + z_im * d_im, z_re * d_im - z_im * d_re, rows_p, cols_q)
    return (operator_out, filter_grad.reshape(1, channels, length))


MESH = pl.DeviceIdType.MESH
BLOCK = 128
CHUNKS = 4
F32 = jnp.float32
BF16 = jnp.bfloat16


def rows_at(start, size):
    return pl.ds(pl.multiple_of(start, size), size)


def kernel(
    q_hbm, k_hbm, v_hbm, taps_hbm, filt_hbm, weight_hbm, grad_hbm,
    out_ref, fgrad_ref,
    streams, halo, taps, filt, weight, grads,
    q_t, g_send, g_recv, g_wide, toep, h_pad, y_tiles, y_send, y_recv,
    acc, d_send, d_recv, d_pad, f_tiles,
    load_sem, halo_ssem, halo_rsem, gather_ssem, gather_rsem, fwd_ssem,
    g_ssem, g_rsem, y_ssem, y_rsem, d_ssem, d_rsem,
):
    n = g_recv.shape[0]
    me, c = lax.axis_index("seq"), lax.axis_index("chan")
    streams_hbm = (q_hbm, k_hbm, v_hbm)
    cols = grads.shape[2] // CHUNKS

    loads = [pltpu.make_async_copy(ref, streams.at[s], load_sem.at[s]) for s, ref in enumerate(streams_hbm)]
    loads.append(pltpu.make_async_copy(taps_hbm, taps, load_sem.at[3]))
    own_grad = pltpu.make_async_copy(grad_hbm, grads.at[c], load_sem.at[4])
    weight_load = pltpu.make_async_copy(weight_hbm, weight, load_sem.at[5])
    filt_loads = [
        pltpu.make_async_copy(filt_hbm.at[0, :, pl.ds(a * BLOCK, BLOCK)], filt.at[a], load_sem.at[6 + a])
        for a in range(n)
    ]
    for copy in (*loads, own_grad, *filt_loads, weight_load):
        copy.start()

    barrier = pltpu.get_barrier_semaphore()
    for r in range(1, n):
        pl.semaphore_signal(barrier, inc=1, device_id=(lax.rem(me + r, n), c), device_id_type=MESH)
    for r in range(1, 4):
        pl.semaphore_signal(barrier, inc=1, device_id=(me, lax.rem(c + r, 4)), device_id_type=MESH)
    pl.semaphore_wait(barrier, n - 1 + 3)

    nxt = lax.rem(me + 1, n)
    halo_copies = [
        pltpu.make_async_remote_copy(
            src_ref=ref.at[pl.ds(BLOCK - 16, 16), :], dst_ref=halo.at[s],
            send_sem=halo_ssem.at[s], recv_sem=halo_rsem.at[s],
            device_id=(nxt, c), device_id_type=MESH,
        )
        for s, ref in enumerate(streams_hbm)
    ]

    @pl.when(me < n - 1)
    def _():
        for copy in halo_copies:
            copy.start()

    @pl.when(me == 0)
    def _():
        halo[...] = jnp.zeros_like(halo)

    partner = c + 1 - 2 * lax.rem(c, 2)
    half = c // 2
    near = 2 - half
    far = 3 - 3 * half
    middle = jnp.logical_or(c == 1, c == 2)

    def gather_copy(block, chunk, src, dst_chan, ssem):
        return pltpu.make_async_remote_copy(
            src_ref=src, dst_ref=grads.at[block, :, pl.ds(chunk * cols, cols)],
            send_sem=ssem, recv_sem=gather_rsem.at[block, chunk],
            device_id=(me, dst_chan), device_id_type=MESH,
        )

    own_sends = []
    for chunk in range(CHUNKS):
        src = grad_hbm.at[:, pl.ds(chunk * cols, cols)]
        own_sends.append(gather_copy(c, chunk, src, partner, gather_ssem.at[0, chunk]))
        own_sends.append(gather_copy(c, chunk, src, near, gather_ssem.at[1, chunk]))
    for copy in own_sends:
        copy.start()

    def forward_copy(which, block, chunk):
        src = grads.at[block, :, pl.ds(chunk * cols, cols)]
        return gather_copy(block, chunk, src, partner, fwd_ssem.at[which, chunk])

    def forward(chunk):
        @pl.when(middle)
        def _():
            for which, block in enumerate((near, far)):
                copy = forward_copy(which, block, chunk)
                copy.wait_recv()
                copy.start()

    for copy in loads:
        copy.wait()

    @pl.when(me > 0)
    def _():
        for copy in halo_copies:
            copy.wait_recv()

    row = lax.broadcasted_iota(jnp.int32, (BLOCK, BLOCK), 0)
    lane = lax.broadcasted_iota(jnp.int32, (BLOCK, BLOCK), 1)
    flip = jnp.where(row + lane == BLOCK - 1, 1.0, 0.0).astype(BF16)

    def exchange(send_ref, recv_ref, ssem, rsem, r):
        return pltpu.make_async_remote_copy(
            src_ref=send_ref.at[lax.rem(me + r, n)], dst_ref=recv_ref.at[me],
            send_sem=ssem.at[r], recv_sem=rsem.at[r],
            device_id=(lax.rem(me + r, n), c), device_id_type=MESH,
        )

    @pl.loop(1, n + 1)
    def _(r):
        p = lax.rem(me + r, n)
        here = rows_at(p * BLOCK, BLOCK)
        conv = []
        for s in range(3):
            value = streams[s, :, here].astype(F32)
            tail = halo[s, :, here].astype(F32)
            total = taps[s, 0:1, here] * value
            one = jnp.where(row == 0, tail[15:16, :], pltpu.roll(value, 1, 0))
            total = total + taps[s, 1:2, here] * one
            two = pltpu.roll(value, 2, 0)
            two = jnp.where(row == 0, tail[14:15, :], jnp.where(row == 1, tail[15:16, :], two))
            conv.append(total + taps[s, 2:3, here] * two)
        q_t[here, :] = conv[0].T
        gated = (conv[1] * conv[2]).astype(BF16).astype(F32)
        turned = jnp.dot(gated.T.astype(BF16), flip, preferred_element_type=F32)
        g_send[p] = turned.astype(BF16)

        @pl.when(r < n)
        def _():
            exchange(g_send, g_recv, g_ssem, g_rsem, r).start()

        @pl.when(r == n)
        def _():
            g_recv[me] = turned.astype(BF16)

    h_pad[...] = jnp.zeros_like(h_pad)
    d_pad[...] = jnp.zeros_like(d_pad)
    for a in range(n):
        filt_loads[a].wait()
        value = filt[a]
        high = value.astype(BF16)
        low = (value - high.astype(F32)).astype(BF16)
        turned = jnp.dot(high, flip, preferred_element_type=F32) + jnp.dot(low, flip, preferred_element_type=F32)
        h_pad[pl.ds(n + a, BLOCK, stride=2 * n), :] = turned

    forward(0)
    for r in range(1, n):
        exchange(g_send, g_recv, g_ssem, g_rsem, r).wait_recv()
    g_wide[...] = g_recv[...].astype(F32)

    lane16 = lax.broadcasted_iota(jnp.int32, (16, BLOCK), 1)
    row16 = lax.broadcasted_iota(jnp.int32, (16, BLOCK), 0)
    keep = [lane16 <= row16 + 16 * k for k in range(BLOCK // 16)]

    def build(pair):
        for side in range(2):
            first = []
            for u in range(n):
                source = jnp.broadcast_to(g_wide[u, pl.ds(pair * 2 + side, 1), :], (16, BLOCK))
                first.append(pltpu.roll(source, 1, 1, stride=1, stride_axis=0).astype(BF16))
            for k in range(BLOCK // 16):
                other = jnp.zeros_like(first[0])
                for u in range(n):
                    turned = pltpu.roll(first[u], 16 * k, 1) if k else first[u]
                    at = u * BLOCK + 16 * k
                    toep[pair, at : at + 16, side * BLOCK : (side + 1) * BLOCK] = jnp.where(keep[k], turned, other)
                    other = turned

    def convolve(pair):
        rows = []
        for side in range(2):
            at = (pair * 2 + side) * 2 * n + n
            left = jnp.concatenate([h_pad[pl.ds(at - u, n), :] for u in range(n)], axis=1)
            high = left.astype(BF16).astype(F32)
            rows += [high, left - high]
        both = jnp.concatenate(rows, axis=0).astype(BF16)
        result = jnp.dot(both, toep[pair], preferred_element_type=F32)
        y_tiles[rows_at(pair * 2 * n, n), :] = result[:n, :BLOCK] + result[n : 2 * n, :BLOCK]
        y_tiles[rows_at(pair * 2 * n + n, n), :] = result[2 * n : 3 * n, BLOCK:] + result[3 * n :, BLOCK:]

    def pairs(first, last):
        @pl.loop(first, last)
        def _(pair):
            convolve(pair - 1)
            build(pair)

    def add_block(at, block):
        if at:
            @pl.when(jnp.logical_or(jnp.logical_not(middle), at == 1))
            def _():
                for chunk in range(CHUNKS):
                    gather_copy(block, chunk, grad_hbm.at[:, pl.ds(chunk * cols, cols)], partner, gather_ssem.at[0, chunk]).wait_recv()

        wide = grads.shape[2]

        @pl.loop(0, 4)
        def _(part):
            size = acc.shape[0] // 4
            here = rows_at(part * size, size)
            term = lax.dot_general(
                weight[here, rows_at(block * wide, wide)], grads[block],
                (((1,), (1,)), ((), ())), preferred_element_type=F32,
            )
            acc[here, :] = term if at == 0 else acc[here, :] + term

    forward(1)
    build(0)
    pairs(1, 16)
    forward(2)
    pairs(16, 32)
    forward(3)
    weight_load.wait()
    own_grad.wait()
    add_block(0, c)
    add_block(1, partner)
    pairs(32, 44)
    add_block(2, near)
    add_block(3, far)
    for r in range(1, n + 1):
        p = lax.rem(me + r, n)
        here = rows_at(p * BLOCK, BLOCK)
        value = (acc[here, :] * q_t[here, :]).astype(BF16)
        if r < n:
            d_send[p] = value
            exchange(d_send, d_recv, d_ssem, d_rsem, r).start()
        else:
            d_recv[me] = value
    pairs(44, BLOCK // 2)
    convolve(BLOCK // 2 - 1)

    for u in range(n):
        y_send[u] = y_tiles[pl.ds(u, BLOCK, stride=n), :].astype(BF16)
    for r in range(1, n):
        exchange(y_send, y_recv, y_ssem, y_rsem, r).start()
    y_recv[me] = y_send[me]

    for r in range(1, n):
        exchange(d_send, d_recv, d_ssem, d_rsem, r).wait_recv()
    for u in range(n):
        d_pad[pl.ds(u, BLOCK, stride=2 * n), :] = d_recv[u].astype(F32)

    @pl.loop(0, BLOCK // 4)
    def _(two):
        for i in range(2):
            pair = two * 2 + i
            rows = []
            for side in range(2):
                at = (pair * 2 + side) * 2 * n
                rows.append(jnp.concatenate([d_pad[pl.ds(at + u, n), :] for u in range(n)], axis=1))
            both = jnp.concatenate(rows, axis=0).astype(BF16)
            result = jnp.dot(both, toep[pair], preferred_element_type=F32)
            f_tiles[rows_at(pair * 2 * n, n), :] = result[:n, :BLOCK]
            f_tiles[rows_at(pair * 2 * n + n, n), :] = result[n:, BLOCK:]

    for s in range(n):
        fgrad_ref[0, :, s * BLOCK : (s + 1) * BLOCK] = f_tiles[pl.ds(s, BLOCK, stride=n), :]

    for r in range(1, n):
        exchange(y_send, y_recv, y_ssem, y_rsem, r).wait_recv()

    @pl.loop(0, n)
    def _(p):
        here = rows_at(p * BLOCK, BLOCK)
        y = jnp.dot(y_recv[p], flip, preferred_element_type=F32)
        out_ref[:, here] = (q_t[here, :] * y).T.astype(BF16)

    @pl.when(me < n - 1)
    def _():
        for copy in halo_copies:
            copy.wait_send()

    for copy in own_sends:
        copy.wait_send()

    @pl.when(middle)
    def _():
        for chunk in range(CHUNKS):
            for which, block in enumerate((near, far)):
                forward_copy(which, block, chunk).wait_send()

    for r in range(1, n):
        exchange(g_send, g_recv, g_ssem, g_rsem, r).wait_send()
        exchange(y_send, y_recv, y_ssem, y_rsem, r).wait_send()
        exchange(d_send, d_recv, d_ssem, d_rsem, r).wait_send()


def on_device(q_in, k_in, v_in, short_filters, long_filter, out_weight, out_grad):
    tokens, group_w = q_in.shape
    taps = short_filters.shape[1]
    channels, length = long_filter.shape[1:]
    n, chans = lax.axis_size("seq"), lax.axis_size("chan")
    fits = (tokens, channels, n, chans, taps, length) == (BLOCK, BLOCK, 8, 4, 3, 8 * BLOCK)
    if not fits or out_weight.shape != (n * BLOCK, chans * group_w):
        return on_device_by_spectrum(q_in, k_in, v_in, short_filters, long_filter, out_weight, out_grad)
    dma = pltpu.SemaphoreType.DMA
    blocks = (n, BLOCK, BLOCK)
    return pl.pallas_call(
        kernel,
        out_shape=(
            jax.ShapeDtypeStruct(q_in.shape, BF16),
            jax.ShapeDtypeStruct(long_filter.shape, F32),
        ),
        in_specs=[pl.BlockSpec(memory_space=pl.ANY)] * 7,
        out_specs=[pl.BlockSpec(memory_space=pltpu.VMEM)] * 2,
        scratch_shapes=[
            pltpu.VMEM((3, tokens, group_w), BF16),
            pltpu.VMEM((3, 16, group_w), BF16),
            pltpu.VMEM(short_filters.shape, F32),
            pltpu.VMEM(blocks, F32),
            pltpu.VMEM(out_weight.shape, BF16),
            pltpu.VMEM((chans, tokens, group_w), BF16),
            pltpu.VMEM((group_w, tokens), F32),
            pltpu.VMEM(blocks, BF16),
            pltpu.VMEM(blocks, BF16),
            pltpu.VMEM(blocks, F32),
            pltpu.VMEM((channels // 2, length, 2 * BLOCK), BF16),
            pltpu.VMEM((channels * 2 * n, BLOCK), F32),
            pltpu.VMEM((channels * n, BLOCK), F32),
            pltpu.VMEM(blocks, BF16),
            pltpu.VMEM(blocks, BF16),
            pltpu.VMEM((group_w, tokens), F32),
            pltpu.VMEM(blocks, BF16),
            pltpu.VMEM(blocks, BF16),
            pltpu.VMEM((channels * 2 * n, BLOCK), F32),
            pltpu.VMEM((channels * n, BLOCK), F32),
            dma((6 + n,)),
            dma((3,)),
            dma((3,)),
            dma((2, CHUNKS)),
            dma((chans, CHUNKS)),
            dma((2, CHUNKS)),
            dma((n,)),
            dma((n,)),
            dma((n,)),
            dma((n,)),
            dma((n,)),
            dma((n,)),
        ],
        compiler_params=pltpu.CompilerParams(
            collective_id=0, has_side_effects=True, vmem_limit_bytes=60 * 1024 * 1024
        ),
    )(q_in, k_in, v_in, short_filters, long_filter, out_weight, out_grad)


def solution(mesh):
    in_specs = (
        P("seq", "chan"),
        P("seq", "chan"),
        P("seq", "chan"),
        P(None, None, "chan"),
        P("chan", "seq", None),
        P("chan", None),
        P("seq", "chan"),
    )
    out_specs = (P("seq", "chan"), P("chan", "seq", None))
    return jax.shard_map(
        on_device, mesh=mesh, in_specs=in_specs, out_specs=out_specs, check_vma=False
    )
```

```python
import functools
import math

import jax
import jax.numpy as jnp
from jax import lax
from jax.experimental import pallas as pl
from jax.experimental.pallas import tpu as pltpu
from jax.sharding import PartitionSpec as P

HIGHEST = lax.Precision.HIGHEST


def shifted(value, axis, steps):
    count = lax.axis_size(axis)
    leading, last = (max(0, -steps), min(count, count - steps))
    return lax.ppermute(value, axis, [(source, source + steps) for source in range(leading, last)])


def angle_table(rows, cols, modulus):
    first = jnp.arange(rows, dtype=jnp.int32)[:, None]
    second = jnp.arange(cols, dtype=jnp.int32)[None, :]
    phase = (first * second % modulus).astype(jnp.float32) * (2.0 * math.pi / modulus)
    return (jnp.cos(phase), jnp.sin(phase))


def spectrum(signal, rows_p, cols_q):
    cos_p, sin_p = angle_table(rows_p // 2, rows_p, rows_p)
    first_re = jnp.einsum("cnq,nk->ckq", signal, cos_p, precision=HIGHEST)
    first_im = -jnp.einsum("cnq,nk->ckq", signal, sin_p, precision=HIGHEST)
    cos_t, sin_t = angle_table(rows_p, cols_q, rows_p * cols_q)
    turn_re = first_re * cos_t + first_im * sin_t
    turn_im = first_im * cos_t - first_re * sin_t
    cos_q, sin_q = angle_table(cols_q, cols_q, cols_q)
    out_re = jnp.einsum("ckq,qm->ckm", turn_re, cos_q, precision=HIGHEST) + jnp.einsum(
        "ckq,qm->ckm", turn_im, sin_q, precision=HIGHEST
    )
    out_im = jnp.einsum("ckq,qm->ckm", turn_im, cos_q, precision=HIGHEST) - jnp.einsum(
        "ckq,qm->ckm", turn_re, sin_q, precision=HIGHEST
    )
    return (out_re, out_im)


def signal_back(spec_re, spec_im, rows_p, cols_q):
    cos_q, sin_q = angle_table(cols_q, cols_q, cols_q)
    mid_re = jnp.einsum("ckm,mq->ckq", spec_re, cos_q, precision=HIGHEST) - jnp.einsum(
        "ckm,mq->ckq", spec_im, sin_q, precision=HIGHEST
    )
    mid_im = jnp.einsum("ckm,mq->ckq", spec_re, sin_q, precision=HIGHEST) + jnp.einsum(
        "ckm,mq->ckq", spec_im, cos_q, precision=HIGHEST
    )
    cos_t, sin_t = angle_table(rows_p, cols_q, rows_p * cols_q)
    turn_re = mid_re * cos_t - mid_im * sin_t
    turn_im = mid_re * sin_t + mid_im * cos_t
    cos_p, sin_p = angle_table(rows_p, rows_p // 2, rows_p)
    real_part = jnp.einsum("ckq,kn->cnq", turn_re, cos_p, precision=HIGHEST) - jnp.einsum(
        "ckq,kn->cnq", turn_im, sin_p, precision=HIGHEST
    )
    return real_part / (rows_p * cols_q)


def regroup(blocked):
    return lax.all_to_all(blocked, "seq", split_axis=0, concat_axis=1, tiled=True)


def on_device_by_spectrum(q_in, k_in, v_in, short_filters, long_filter, out_weight, out_grad):
    tokens, group_w = q_in.shape
    taps = short_filters.shape[1]
    streams = jnp.stack((q_in, k_in, v_in))
    before = shifted(streams[:, tokens - (taps - 1) :, :], "seq", 1)
    extended = jnp.concatenate((before, streams), axis=1).astype(jnp.float32)
    conv = short_filters[:, 0, None, :] * extended[:, taps - 1 : taps - 1 + tokens, :]
    for lag in range(1, taps):
        conv = (
            conv
            + short_filters[:, lag, None, :]
            * extended[:, taps - 1 - lag : taps - 1 - lag + tokens, :]
        )
    q_conv = conv[0]
    gated_t = (conv[1] * conv[2]).astype(jnp.bfloat16).T
    channels = long_filter.shape[1]
    length = long_filter.shape[2]
    cols_q = length // tokens
    rows_p = 2 * tokens
    filters = long_filter.reshape(channels, tokens, cols_q)
    z_chan = regroup(gated_t)
    z_re, z_im = spectrum(
        z_chan.astype(jnp.float32).reshape(channels, tokens, cols_q), rows_p, cols_q
    )
    h_re, h_im = spectrum(filters, rows_p, cols_q)
    y_chan = signal_back(z_re * h_re - z_im * h_im, z_re * h_im + z_im * h_re, rows_p, cols_q)
    y_chan = y_chan.reshape(channels, length).astype(jnp.bfloat16)
    y_tok = lax.all_to_all(y_chan, "seq", split_axis=1, concat_axis=0, tiled=True)
    operator_out = (q_conv * y_tok.T.astype(jnp.float32)).astype(jnp.bfloat16)
    grad_gate = jnp.einsum(
        "tw,iw->ti",
        lax.all_gather(out_grad, "chan", axis=1, tiled=True),
        out_weight,
        preferred_element_type=jnp.float32,
    )
    dy_chan = regroup((grad_gate * q_conv).astype(jnp.bfloat16).T)
    d_re, d_im = spectrum(
        dy_chan.astype(jnp.float32).reshape(channels, tokens, cols_q), rows_p, cols_q
    )
    filter_grad = signal_back(z_re * d_re + z_im * d_im, z_re * d_im - z_im * d_re, rows_p, cols_q)
    return (operator_out, filter_grad.reshape(1, channels, length))


MESH = pl.DeviceIdType.MESH
BLOCK = 128
CHUNKS = 4
GROUP = 8
F32 = jnp.float32
BF16 = jnp.bfloat16


def rows_at(start, size):
    return pl.ds(pl.multiple_of(start, size), size)


def kernel(
    q_hbm, k_hbm, v_hbm, taps_hbm, filt_hbm, weight_hbm, grad_hbm,
    out_ref, fgrad_ref,
    streams, halo, taps, filt, weight, grads,
    q_t, g_send, g_recv, g_wide, toep, h_pad, h_left, y_tiles, y_send, y_recv,
    acc, d_send, d_recv, d_pad, d_even, d_odd, f_tiles,
    load_sem, halo_ssem, halo_rsem, gather_ssem, gather_rsem, fwd_ssem,
    g_ssem, g_rsem, y_ssem, y_rsem, d_ssem, d_rsem,
):
    n = g_recv.shape[0]
    me, c = lax.axis_index("seq"), lax.axis_index("chan")
    streams_hbm = (q_hbm, k_hbm, v_hbm)
    cols = grads.shape[2] // CHUNKS

    loads = [pltpu.make_async_copy(ref, streams.at[s], load_sem.at[s]) for s, ref in enumerate(streams_hbm)]
    loads.append(pltpu.make_async_copy(taps_hbm, taps, load_sem.at[3]))
    own_grad = pltpu.make_async_copy(grad_hbm, grads.at[c], load_sem.at[4])
    weight_load = pltpu.make_async_copy(weight_hbm, weight, load_sem.at[5])
    filt_loads = [
        pltpu.make_async_copy(filt_hbm.at[0, :, pl.ds(a * BLOCK, BLOCK)], filt.at[a], load_sem.at[6 + a])
        for a in range(n)
    ]
    for copy in (*loads, own_grad, *filt_loads, weight_load):
        copy.start()

    barrier = pltpu.get_barrier_semaphore()
    for r in range(1, n):
        pl.semaphore_signal(barrier, inc=1, device_id=(lax.rem(me + r, n), c), device_id_type=MESH)
    for r in range(1, 4):
        pl.semaphore_signal(barrier, inc=1, device_id=(me, lax.rem(c + r, 4)), device_id_type=MESH)
    pl.semaphore_wait(barrier, n - 1 + 3)

    nxt = lax.rem(me + 1, n)
    halo_copies = [
        pltpu.make_async_remote_copy(
            src_ref=ref.at[pl.ds(BLOCK - 16, 16), :], dst_ref=halo.at[s],
            send_sem=halo_ssem.at[s], recv_sem=halo_rsem.at[s],
            device_id=(nxt, c), device_id_type=MESH,
        )
        for s, ref in enumerate(streams_hbm)
    ]

    @pl.when(me < n - 1)
    def _():
        for copy in halo_copies:
            copy.start()

    @pl.when(me == 0)
    def _():
        halo[...] = jnp.zeros_like(halo)

    partner = c + 1 - 2 * lax.rem(c, 2)
    half = c // 2
    near = 2 - half
    far = 3 - 3 * half
    middle = jnp.logical_or(c == 1, c == 2)

    def gather_copy(block, chunk, src, dst_chan, ssem):
        return pltpu.make_async_remote_copy(
            src_ref=src, dst_ref=grads.at[block, :, pl.ds(chunk * cols, cols)],
            send_sem=ssem, recv_sem=gather_rsem.at[block, chunk],
            device_id=(me, dst_chan), device_id_type=MESH,
        )

    own_sends = []
    for chunk in range(CHUNKS):
        src = grad_hbm.at[:, pl.ds(chunk * cols, cols)]
        own_sends.append(gather_copy(c, chunk, src, partner, gather_ssem.at[0, chunk]))
        own_sends.append(gather_copy(c, chunk, src, near, gather_ssem.at[1, chunk]))
    for copy in own_sends:
        copy.start()

    def forward_copy(which, block, chunk):
        src = grads.at[block, :, pl.ds(chunk * cols, cols)]
        return gather_copy(block, chunk, src, partner, fwd_ssem.at[which, chunk])

    def forward(chunk):
        @pl.when(middle)
        def _():
            for which, block in enumerate((near, far)):
                copy = forward_copy(which, block, chunk)
                copy.wait_recv()
                copy.start()

    row = lax.broadcasted_iota(jnp.int32, (BLOCK, BLOCK), 0)
    lane = lax.broadcasted_iota(jnp.int32, (BLOCK, BLOCK), 1)
    flip = jnp.where(row + lane == BLOCK - 1, 1.0, 0.0).astype(BF16)

    def lay_out(pad, blocks):
        pad[...] = jnp.zeros_like(pad)
        for r in range(4):
            turned = [pltpu.roll(x, BLOCK - 32 * r, 1) if r else x for x in blocks]
            for a in range(n):
                value = turned[a]
                if r:
                    after = turned[a + 1] if a + 1 < n else jnp.zeros_like(value)
                    value = jnp.where(lane < BLOCK - 32 * r, value, after)
                pad[r, pl.ds(a, BLOCK, stride=2 * n), :] = value

    def left_rows(pad, channel, r, u):
        at = channel * 2 * n
        return jnp.concatenate([pad[r, pl.ds(at + u, n), :], pad[r + 1, pl.ds(at + u, n), :]], axis=0)

    blocks = []
    for a in reversed(range(n)):
        filt_loads[a].wait()
        value = filt[a]
        high = value.astype(BF16)
        low = (value - high.astype(F32)).astype(BF16)
        blocks.append(
            jnp.dot(high, flip, preferred_element_type=F32) + jnp.dot(low, flip, preferred_element_type=F32)
        )
    lay_out(h_pad, blocks)

    @pl.loop(0, BLOCK // GROUP)
    def _(group):
        for j in range(GROUP):
            for r in (0, 2):
                for u in range(n):
                    value = left_rows(h_pad, group * GROUP + j, r, u)
                    high = value.astype(BF16)
                    at = 32 * j + 8 * r
                    here = slice(u * BLOCK, (u + 1) * BLOCK)
                    h_left[group, at : at + 16, here] = high
                    h_left[group, 256 + at : 256 + at + 16, here] = (value - high.astype(F32)).astype(BF16)

    for copy in loads:
        copy.wait()

    @pl.when(me > 0)
    def _():
        for copy in halo_copies:
            copy.wait_recv()

    def exchange(send_ref, recv_ref, ssem, rsem, r):
        return pltpu.make_async_remote_copy(
            src_ref=send_ref.at[lax.rem(me + r, n)], dst_ref=recv_ref.at[me],
            send_sem=ssem.at[r], recv_sem=rsem.at[r],
            device_id=(lax.rem(me + r, n), c), device_id_type=MESH,
        )

    for r in range(1, n + 1):
        p = lax.rem(me + r, n)
        here = rows_at(p * BLOCK, BLOCK)
        conv = []
        for s in range(3):
            value = streams[s, :, here].astype(F32)
            tail = halo[s, :, here].astype(F32)
            total = taps[s, 0:1, here] * value
            one = jnp.where(row == 0, tail[15:16, :], pltpu.roll(value, 1, 0))
            total = total + taps[s, 1:2, here] * one
            two = pltpu.roll(value, 2, 0)
            two = jnp.where(row == 0, tail[14:15, :], jnp.where(row == 1, tail[15:16, :], two))
            conv.append(total + taps[s, 2:3, here] * two)
        q_t[here, :] = conv[0].T
        gated = (conv[1] * conv[2]).T.astype(BF16)
        if r < n:
            g_send[p] = gated
            exchange(g_send, g_recv, g_ssem, g_rsem, r).start()
        else:
            g_recv[me] = gated

    forward(0)
    for r in range(1, n):
        exchange(g_send, g_recv, g_ssem, g_rsem, r).wait_recv()
    g_wide[...] = g_recv[...].astype(F32)

    lane16 = lax.broadcasted_iota(jnp.int32, (16, BLOCK), 1)
    row16 = lax.broadcasted_iota(jnp.int32, (16, BLOCK), 0)
    keep = [lane16 >= row16 + 16 * k for k in range(2)]
    strip = lax.broadcasted_iota(jnp.int32, (n, BLOCK), 1) // 32

    def build(group):
        for j in range(GROUP):
            other = [jnp.zeros((16, BLOCK), BF16)] * 2
            for u in range(n):
                source = jnp.broadcast_to(g_wide[u, pl.ds(group * GROUP + j, 1), :], (16, BLOCK))
                first = pltpu.roll(source, 0, 1, stride=1, stride_axis=0).astype(BF16)
                turned = [first, pltpu.roll(first, 16, 1)]
                for k in range(2):
                    at = 32 * j + 16 * k
                    toep[group, at : at + 16, u * BLOCK : (u + 1) * BLOCK] = jnp.where(keep[k], turned[k], other[k])
                other = turned

    def correlate(left, group):
        return lax.dot_general(left, toep[group], (((1,), (1,)), ((), ())), preferred_element_type=F32)

    def put(tiles, group, result):
        for j in range(GROUP):
            half = j // 4 * BLOCK
            tile = None
            for r in range(4):
                piece = result[32 * j + 8 * r : 32 * j + 8 * r + 8, half : half + BLOCK]
                turn = 32 * (r - j % 4) % BLOCK
                piece = pltpu.roll(piece, turn, 1) if turn else piece
                tile = jnp.where(strip == r, piece, tile) if r else piece
            tiles[rows_at(group * GROUP * n + j * n, n), :] = tile

    def convolve(group):
        result = correlate(h_left[group], group)
        put(y_tiles, group, result[:256] + result[256:])

    def groups(first, last):
        @pl.loop(first, last)
        def _(group):
            convolve(group - 1)
            build(group)

    def add_block(at, block):
        if at:
            @pl.when(jnp.logical_or(jnp.logical_not(middle), at == 1))
            def _():
                for chunk in range(CHUNKS):
                    gather_copy(block, chunk, grad_hbm.at[:, pl.ds(chunk * cols, cols)], partner, gather_ssem.at[0, chunk]).wait_recv()

        wide = grads.shape[2]

        @pl.loop(0, 2)
        def _(part):
            size = acc.shape[0] // 2
            here = rows_at(part * size, size)
            term = lax.dot_general(
                weight[here, rows_at(block * wide, wide)], grads[block],
                (((1,), (1,)), ((), ())), preferred_element_type=F32,
            )
            acc[here, :] = term if at == 0 else acc[here, :] + term

    forward(1)
    build(0)
    groups(1, 4)
    forward(2)
    groups(4, 8)
    forward(3)
    weight_load.wait()
    own_grad.wait()
    add_block(0, c)
    add_block(1, partner)
    groups(8, 11)
    add_block(2, near)
    add_block(3, far)
    for r in range(1, n + 1):
        p = lax.rem(me + r, n)
        here = rows_at(p * BLOCK, BLOCK)
        value = (acc[here, :] * q_t[here, :]).astype(BF16)
        if r < n:
            d_send[p] = value
            exchange(d_send, d_recv, d_ssem, d_rsem, r).start()
        else:
            d_recv[me] = value
    groups(11, BLOCK // GROUP)
    convolve(BLOCK // GROUP - 1)

    for u in range(n):
        y_send[u] = y_tiles[pl.ds(n - 1 - u, BLOCK, stride=n), :].astype(BF16)
    for r in range(1, n):
        exchange(y_send, y_recv, y_ssem, y_rsem, r).start()
    y_recv[me] = y_send[me]

    for r in range(1, n):
        exchange(d_send, d_recv, d_ssem, d_rsem, r).wait_recv()
    lay_out(d_pad, [d_recv[u].astype(F32) for u in range(n)])

    def fill(left, group):
        for j in range(GROUP):
            for r in (0, 2):
                for u in range(n):
                    at = 32 * j + 8 * r
                    value = left_rows(d_pad, group * GROUP + j, r, u)
                    left[at : at + 16, u * BLOCK : (u + 1) * BLOCK] = value.astype(BF16)

    last = BLOCK // GROUP - 1
    fill(d_even, 0)

    @pl.loop(0, BLOCK // GROUP // 2)
    def _(two):
        group = two * 2
        result = correlate(d_even[...], group)
        fill(d_odd, group + 1)
        put(f_tiles, group, result)
        result = correlate(d_odd[...], group + 1)
        fill(d_even, jnp.minimum(group + 2, last))
        put(f_tiles, group + 1, result)

    for s in range(n):
        fgrad_ref[0, :, s * BLOCK : (s + 1) * BLOCK] = f_tiles[pl.ds(s, BLOCK, stride=n), :]

    for r in range(1, n):
        exchange(y_send, y_recv, y_ssem, y_rsem, r).wait_recv()

    @pl.loop(0, n)
    def _(p):
        here = rows_at(p * BLOCK, BLOCK)
        y = jnp.dot(y_recv[p], flip, preferred_element_type=F32)
        out_ref[:, here] = (q_t[here, :] * y).T.astype(BF16)

    @pl.when(me < n - 1)
    def _():
        for copy in halo_copies:
            copy.wait_send()

    for copy in own_sends:
        copy.wait_send()

    @pl.when(middle)
    def _():
        for chunk in range(CHUNKS):
            for which, block in enumerate((near, far)):
                forward_copy(which, block, chunk).wait_send()

    for r in range(1, n):
        exchange(g_send, g_recv, g_ssem, g_rsem, r).wait_send()
        exchange(y_send, y_recv, y_ssem, y_rsem, r).wait_send()
        exchange(d_send, d_recv, d_ssem, d_rsem, r).wait_send()


def on_device(q_in, k_in, v_in, short_filters, long_filter, out_weight, out_grad):
    tokens, group_w = q_in.shape
    taps = short_filters.shape[1]
    channels, length = long_filter.shape[1:]
    n, chans = lax.axis_size("seq"), lax.axis_size("chan")
    fits = (tokens, channels, n, chans, taps, length) == (BLOCK, BLOCK, 8, 4, 3, 8 * BLOCK)
    if not fits or out_weight.shape != (n * BLOCK, chans * group_w):
        return on_device_by_spectrum(q_in, k_in, v_in, short_filters, long_filter, out_weight, out_grad)
    dma = pltpu.SemaphoreType.DMA
    blocks = (n, BLOCK, BLOCK)
    return pl.pallas_call(
        kernel,
        out_shape=(
            jax.ShapeDtypeStruct(q_in.shape, BF16),
            jax.ShapeDtypeStruct(long_filter.shape, F32),
        ),
        in_specs=[pl.BlockSpec(memory_space=pl.ANY)] * 7,
        out_specs=[pl.BlockSpec(memory_space=pltpu.VMEM)] * 2,
        scratch_shapes=[
            pltpu.VMEM((3, tokens, group_w), BF16),
            pltpu.VMEM((3, 16, group_w), BF16),
            pltpu.VMEM(short_filters.shape, F32),
            pltpu.VMEM(blocks, F32),
            pltpu.VMEM(out_weight.shape, BF16),
            pltpu.VMEM((chans, tokens, group_w), BF16),
            pltpu.VMEM((group_w, tokens), F32),
            pltpu.VMEM(blocks, BF16),
            pltpu.VMEM(blocks, BF16),
            pltpu.VMEM(blocks, F32),
            pltpu.VMEM((channels // GROUP, 32 * GROUP, length), BF16),
            pltpu.VMEM((4, channels * 2 * n, BLOCK), F32),
            pltpu.VMEM((channels // GROUP, 64 * GROUP, length), BF16),
            pltpu.VMEM((channels * n, BLOCK), F32),
            pltpu.VMEM(blocks, BF16),
            pltpu.VMEM(blocks, BF16),
            pltpu.VMEM((group_w, tokens), F32),
            pltpu.VMEM(blocks, BF16),
            pltpu.VMEM(blocks, BF16),
            pltpu.VMEM((4, channels * 2 * n, BLOCK), F32),
            pltpu.VMEM((32 * GROUP, length), BF16),
            pltpu.VMEM((32 * GROUP, length), BF16),
            pltpu.VMEM((channels * n, BLOCK), F32),
            dma((6 + n,)),
            dma((3,)),
            dma((3,)),
            dma((2, CHUNKS)),
            dma((chans, CHUNKS)),
            dma((2, CHUNKS)),
            dma((n,)),
            dma((n,)),
            dma((n,)),
            dma((n,)),
            dma((n,)),
            dma((n,)),
        ],
        compiler_params=pltpu.CompilerParams(
            collective_id=0, has_side_effects=True, vmem_limit_bytes=60 * 1024 * 1024
        ),
    )(q_in, k_in, v_in, short_filters, long_filter, out_weight, out_grad)


def solution(mesh):
    in_specs = (
        P("seq", "chan"),
        P("seq", "chan"),
        P("seq", "chan"),
        P(None, None, "chan"),
        P("chan", "seq", None),
        P("chan", None),
        P("seq", "chan"),
    )
    out_specs = (P("seq", "chan"), P("chan", "seq", None))
    return jax.shard_map(
        on_device, mesh=mesh, in_specs=in_specs, out_specs=out_specs, check_vma=False
    )
```

```python
import functools
import math

import jax
import jax.numpy as jnp
from jax import lax
from jax.experimental import pallas as pl
from jax.experimental.pallas import tpu as pltpu
from jax.sharding import PartitionSpec as P

HIGHEST = lax.Precision.HIGHEST


def shifted(value, axis, steps):
    count = lax.axis_size(axis)
    leading, last = (max(0, -steps), min(count, count - steps))
    return lax.ppermute(value, axis, [(source, source + steps) for source in range(leading, last)])


def angle_table(rows, cols, modulus):
    first = jnp.arange(rows, dtype=jnp.int32)[:, None]
    second = jnp.arange(cols, dtype=jnp.int32)[None, :]
    phase = (first * second % modulus).astype(jnp.float32) * (2.0 * math.pi / modulus)
    return (jnp.cos(phase), jnp.sin(phase))


def spectrum(signal, rows_p, cols_q):
    cos_p, sin_p = angle_table(rows_p // 2, rows_p, rows_p)
    first_re = jnp.einsum("cnq,nk->ckq", signal, cos_p, precision=HIGHEST)
    first_im = -jnp.einsum("cnq,nk->ckq", signal, sin_p, precision=HIGHEST)
    cos_t, sin_t = angle_table(rows_p, cols_q, rows_p * cols_q)
    turn_re = first_re * cos_t + first_im * sin_t
    turn_im = first_im * cos_t - first_re * sin_t
    cos_q, sin_q = angle_table(cols_q, cols_q, cols_q)
    out_re = jnp.einsum("ckq,qm->ckm", turn_re, cos_q, precision=HIGHEST) + jnp.einsum(
        "ckq,qm->ckm", turn_im, sin_q, precision=HIGHEST
    )
    out_im = jnp.einsum("ckq,qm->ckm", turn_im, cos_q, precision=HIGHEST) - jnp.einsum(
        "ckq,qm->ckm", turn_re, sin_q, precision=HIGHEST
    )
    return (out_re, out_im)


def signal_back(spec_re, spec_im, rows_p, cols_q):
    cos_q, sin_q = angle_table(cols_q, cols_q, cols_q)
    mid_re = jnp.einsum("ckm,mq->ckq", spec_re, cos_q, precision=HIGHEST) - jnp.einsum(
        "ckm,mq->ckq", spec_im, sin_q, precision=HIGHEST
    )
    mid_im = jnp.einsum("ckm,mq->ckq", spec_re, sin_q, precision=HIGHEST) + jnp.einsum(
        "ckm,mq->ckq", spec_im, cos_q, precision=HIGHEST
    )
    cos_t, sin_t = angle_table(rows_p, cols_q, rows_p * cols_q)
    turn_re = mid_re * cos_t - mid_im * sin_t
    turn_im = mid_re * sin_t + mid_im * cos_t
    cos_p, sin_p = angle_table(rows_p, rows_p // 2, rows_p)
    real_part = jnp.einsum("ckq,kn->cnq", turn_re, cos_p, precision=HIGHEST) - jnp.einsum(
        "ckq,kn->cnq", turn_im, sin_p, precision=HIGHEST
    )
    return real_part / (rows_p * cols_q)


def regroup(blocked):
    return lax.all_to_all(blocked, "seq", split_axis=0, concat_axis=1, tiled=True)


def on_device_by_spectrum(q_in, k_in, v_in, short_filters, long_filter, out_weight, out_grad):
    tokens, group_w = q_in.shape
    taps = short_filters.shape[1]
    streams = jnp.stack((q_in, k_in, v_in))
    before = shifted(streams[:, tokens - (taps - 1) :, :], "seq", 1)
    extended = jnp.concatenate((before, streams), axis=1).astype(jnp.float32)
    conv = short_filters[:, 0, None, :] * extended[:, taps - 1 : taps - 1 + tokens, :]
    for lag in range(1, taps):
        conv = (
            conv
            + short_filters[:, lag, None, :]
            * extended[:, taps - 1 - lag : taps - 1 - lag + tokens, :]
        )
    q_conv = conv[0]
    gated_t = (conv[1] * conv[2]).astype(jnp.bfloat16).T
    channels = long_filter.shape[1]
    length = long_filter.shape[2]
    cols_q = length // tokens
    rows_p = 2 * tokens
    filters = long_filter.reshape(channels, tokens, cols_q)
    z_chan = regroup(gated_t)
    z_re, z_im = spectrum(
        z_chan.astype(jnp.float32).reshape(channels, tokens, cols_q), rows_p, cols_q
    )
    h_re, h_im = spectrum(filters, rows_p, cols_q)
    y_chan = signal_back(z_re * h_re - z_im * h_im, z_re * h_im + z_im * h_re, rows_p, cols_q)
    y_chan = y_chan.reshape(channels, length).astype(jnp.bfloat16)
    y_tok = lax.all_to_all(y_chan, "seq", split_axis=1, concat_axis=0, tiled=True)
    operator_out = (q_conv * y_tok.T.astype(jnp.float32)).astype(jnp.bfloat16)
    grad_gate = jnp.einsum(
        "tw,iw->ti",
        lax.all_gather(out_grad, "chan", axis=1, tiled=True),
        out_weight,
        preferred_element_type=jnp.float32,
    )
    dy_chan = regroup((grad_gate * q_conv).astype(jnp.bfloat16).T)
    d_re, d_im = spectrum(
        dy_chan.astype(jnp.float32).reshape(channels, tokens, cols_q), rows_p, cols_q
    )
    filter_grad = signal_back(z_re * d_re + z_im * d_im, z_re * d_im - z_im * d_re, rows_p, cols_q)
    return (operator_out, filter_grad.reshape(1, channels, length))


MESH = pl.DeviceIdType.MESH
BLOCK = 128
CHUNKS = 4
GROUP = 8
F32 = jnp.float32
BF16 = jnp.bfloat16


def rows_at(start, size):
    return pl.ds(pl.multiple_of(start, size), size)


def kernel(
    q_hbm, k_hbm, v_hbm, taps_hbm, filt_hbm, weight_hbm, grad_hbm,
    out_ref, fgrad_ref,
    streams, halo, taps, filt, weight, grads,
    q_t, g_send, g_recv, g_wide, toep, h_rev, y_tiles, y_send, y_recv,
    acc, d_send, d_recv, fold, left_even, left_odd,
    load_sem, halo_ssem, halo_rsem, gather_ssem, gather_rsem, fwd_ssem,
    g_ssem, g_rsem, y_ssem, y_rsem, d_ssem, d_rsem,
):
    n = g_recv.shape[0]
    me, c = lax.axis_index("seq"), lax.axis_index("chan")
    streams_hbm = (q_hbm, k_hbm, v_hbm)
    cols = grads.shape[2] // CHUNKS

    loads = [pltpu.make_async_copy(ref, streams.at[s], load_sem.at[s]) for s, ref in enumerate(streams_hbm)]
    loads.append(pltpu.make_async_copy(taps_hbm, taps, load_sem.at[3]))
    own_grad = pltpu.make_async_copy(grad_hbm, grads.at[c], load_sem.at[4])
    weight_load = pltpu.make_async_copy(weight_hbm, weight, load_sem.at[5])
    filt_loads = [
        pltpu.make_async_copy(filt_hbm.at[0, :, pl.ds(a * BLOCK, BLOCK)], filt.at[a], load_sem.at[6 + a])
        for a in range(n)
    ]
    for copy in (*loads, own_grad, *filt_loads, weight_load):
        copy.start()

    barrier = pltpu.get_barrier_semaphore()
    for r in range(1, n):
        pl.semaphore_signal(barrier, inc=1, device_id=(lax.rem(me + r, n), c), device_id_type=MESH)
    for r in range(1, 4):
        pl.semaphore_signal(barrier, inc=1, device_id=(me, lax.rem(c + r, 4)), device_id_type=MESH)
    pl.semaphore_wait(barrier, n - 1 + 3)

    nxt = lax.rem(me + 1, n)
    halo_copies = [
        pltpu.make_async_remote_copy(
            src_ref=ref.at[pl.ds(BLOCK - 16, 16), :], dst_ref=halo.at[s],
            send_sem=halo_ssem.at[s], recv_sem=halo_rsem.at[s],
            device_id=(nxt, c), device_id_type=MESH,
        )
        for s, ref in enumerate(streams_hbm)
    ]

    @pl.when(me < n - 1)
    def _():
        for copy in halo_copies:
            copy.start()

    @pl.when(me == 0)
    def _():
        halo[...] = jnp.zeros_like(halo)

    partner = c + 1 - 2 * lax.rem(c, 2)
    half = c // 2
    near = 2 - half
    far = 3 - 3 * half
    middle = jnp.logical_or(c == 1, c == 2)

    def gather_copy(block, chunk, src, dst_chan, ssem):
        return pltpu.make_async_remote_copy(
            src_ref=src, dst_ref=grads.at[block, :, pl.ds(chunk * cols, cols)],
            send_sem=ssem, recv_sem=gather_rsem.at[block, chunk],
            device_id=(me, dst_chan), device_id_type=MESH,
        )

    own_sends = []
    for chunk in range(CHUNKS):
        src = grad_hbm.at[:, pl.ds(chunk * cols, cols)]
        own_sends.append(gather_copy(c, chunk, src, partner, gather_ssem.at[0, chunk]))
        own_sends.append(gather_copy(c, chunk, src, near, gather_ssem.at[1, chunk]))
    for copy in own_sends:
        copy.start()

    def forward_copy(which, block, chunk):
        src = grads.at[block, :, pl.ds(chunk * cols, cols)]
        return gather_copy(block, chunk, src, partner, fwd_ssem.at[which, chunk])

    def forward(chunk):
        @pl.when(middle)
        def _():
            for which, block in enumerate((near, far)):
                copy = forward_copy(which, block, chunk)
                copy.wait_recv()
                copy.start()

    row = lax.broadcasted_iota(jnp.int32, (BLOCK, BLOCK), 0)
    lane = lax.broadcasted_iota(jnp.int32, (BLOCK, BLOCK), 1)
    flip = jnp.where(row + lane == BLOCK - 1, 1.0, 0.0).astype(BF16)

    def advance(tiles):
        pairs = []
        lane8 = lane[:8]
        for r in range(4):
            turned = [pltpu.roll(x, BLOCK - 32 * r, 1) if r else x for x in tiles]
            if r:
                after = turned[1:] + [jnp.zeros_like(turned[0])]
                turned = [jnp.where(lane8 < BLOCK - 32 * r, x, y) for x, y in zip(turned, after)]
            turned.append(jnp.zeros_like(turned[0]))
            pairs.append([jnp.concatenate(turned[v : v + 2], axis=0) for v in range(n)])
        return pairs

    def fill(left, first_row, pairs):
        for r in range(4):
            for v in range(n):
                value = pairs[r][v].astype(BF16)
                for m in range(v // 2 + 1):
                    at = first_row + (m * 4 + r) * 16
                    left[at : at + 16, (v - 2 * m) * BLOCK : (v - 2 * m + 1) * BLOCK] = value

    left_even[...] = jnp.zeros_like(left_even)
    left_odd[...] = jnp.zeros_like(left_odd)
    size = fold.shape[0]
    fold_row = lax.broadcasted_iota(jnp.int32, (size, BLOCK), 0) // GROUP
    fold[...] = jnp.where(fold_row == lax.broadcasted_iota(jnp.int32, (size, BLOCK), 1), 1.0, 0.0).astype(BF16)

    for a in range(n):
        filt_loads[a].wait()
        value = filt[a]
        high = value.astype(BF16)
        low = (value - high.astype(F32)).astype(BF16)
        turned = jnp.dot(high, flip, preferred_element_type=F32) + jnp.dot(low, flip, preferred_element_type=F32)
        h_rev[n - 1 - a] = turned

    for copy in loads:
        copy.wait()

    @pl.when(me > 0)
    def _():
        for copy in halo_copies:
            copy.wait_recv()

    def exchange(send_ref, recv_ref, ssem, rsem, r):
        return pltpu.make_async_remote_copy(
            src_ref=send_ref.at[lax.rem(me + r, n)], dst_ref=recv_ref.at[me],
            send_sem=ssem.at[r], recv_sem=rsem.at[r],
            device_id=(lax.rem(me + r, n), c), device_id_type=MESH,
        )

    for r in range(1, n + 1):
        p = lax.rem(me + r, n)
        here = rows_at(p * BLOCK, BLOCK)
        conv = []
        for s in range(3):
            value = streams[s, :, here].astype(F32)
            tail = halo[s, :, here].astype(F32)
            total = taps[s, 0:1, here] * value
            one = jnp.where(row == 0, tail[15:16, :], pltpu.roll(value, 1, 0))
            total = total + taps[s, 1:2, here] * one
            two = pltpu.roll(value, 2, 0)
            two = jnp.where(row == 0, tail[14:15, :], jnp.where(row == 1, tail[15:16, :], two))
            conv.append(total + taps[s, 2:3, here] * two)
        q_t[here, :] = conv[0].T
        gated = (conv[1] * conv[2]).T.astype(BF16)
        if r < n:
            g_send[p] = gated
            exchange(g_send, g_recv, g_ssem, g_rsem, r).start()
        else:
            g_recv[me] = gated

    lane16 = lax.broadcasted_iota(jnp.int32, (16, BLOCK), 1)
    late = lane16 - lax.broadcasted_iota(jnp.int32, (16, BLOCK), 0) // GROUP

    def build(group):
        pairs = []
        for u in range(n):
            value = g_wide[u, rows_at(group * GROUP, GROUP), :]
            pairs.append(jnp.concatenate([value, pltpu.roll(value, 1, 1)], axis=0).astype(BF16))
        for two in range(16):
            keep = late >= 2 * two
            other = jnp.zeros((16, BLOCK), BF16)
            for u in range(n):
                turned = pltpu.roll(pairs[u], 2 * two, 1) if two else pairs[u]
                toep[group, 16 * two : 16 * two + 16, u * BLOCK : (u + 1) * BLOCK] = jnp.where(keep, turned, other)
                other = turned

    def correlate(left, group):
        return lax.dot_general(left, toep[group], (((1,), (1,)), ((), ())), preferred_element_type=F32)

    shape = (16, 2 * BLOCK)
    own = lax.broadcasted_iota(jnp.int32, shape, 0) % GROUP == lax.broadcasted_iota(jnp.int32, shape, 1) % GROUP

    def gather_own(result):
        highs, lows = [], []
        for m in range(4):
            high, low = [], []
            for r in range(4):
                at = (m * 4 + r) * 16
                value = jnp.where(own, result[at : at + 16], 0.0)
                high.append(value.astype(BF16))
                low.append((value - high[-1].astype(F32)).astype(BF16))
            highs.append(jnp.concatenate(high, axis=1))
            lows.append(jnp.concatenate(low, axis=1))
        parts = jnp.concatenate(highs + lows, axis=0)
        folded = jnp.dot(parts, fold[...], preferred_element_type=F32)
        return folded[: 8 * n] + folded[8 * n :]

    def fill_filter(left, group):
        pairs = advance([h_rev[v, rows_at(group * GROUP, GROUP), :] for v in range(n)])
        fill(left, 0, pairs)
        fill(left, 256, [[x - x.astype(BF16).astype(F32) for x in row_of] for row_of in pairs])

    def convolve(left, group):
        result = correlate(left[...], group)
        folded = gather_own(result[:256] + result[256:])
        for s in range(n):
            y_tiles[n - 1 - s, rows_at(group * GROUP, GROUP), :] = folded[s * GROUP : (s + 1) * GROUP]

    last = BLOCK // GROUP - 1

    def groups(first, end):
        @pl.loop(first // 2, end // 2)
        def _(two):
            group = two * 2
            convolve(left_even, group)
            fill_filter(left_odd, group + 1)
            build(group + 1)
            convolve(left_odd, group + 1)
            fill_filter(left_even, jnp.minimum(group + 2, last))
            build(jnp.minimum(group + 2, last))

    def add_block(at, block):
        if at:
            @pl.when(jnp.logical_or(jnp.logical_not(middle), at == 1))
            def _():
                for chunk in range(CHUNKS):
                    gather_copy(block, chunk, grad_hbm.at[:, pl.ds(chunk * cols, cols)], partner, gather_ssem.at[0, chunk]).wait_recv()

        wide = grads.shape[2]

        @pl.loop(0, 2)
        def _(part):
            size = acc.shape[0] // 2
            here = rows_at(part * size, size)
            term = lax.dot_general(
                weight[here, rows_at(block * wide, wide)], grads[block],
                (((1,), (1,)), ((), ())), preferred_element_type=F32,
            )
            acc[here, :] = term if at == 0 else acc[here, :] + term

    weight_load.wait()
    own_grad.wait()
    add_block(0, c)
    fill_filter(left_even, 0)
    forward(0)
    for r in range(1, n):
        exchange(g_send, g_recv, g_ssem, g_rsem, r).wait_recv()
    g_wide[...] = g_recv[...].astype(F32)

    forward(1)
    build(0)
    groups(0, 4)
    forward(2)
    groups(4, 8)
    forward(3)
    add_block(1, partner)
    groups(8, 12)
    add_block(2, near)
    add_block(3, far)
    for r in range(1, n + 1):
        p = lax.rem(me + r, n)
        here = rows_at(p * BLOCK, BLOCK)
        value = (acc[here, :] * q_t[here, :]).astype(BF16)
        if r < n:
            d_send[p] = value
            exchange(d_send, d_recv, d_ssem, d_rsem, r).start()
        else:
            d_recv[me] = value
    groups(12, BLOCK // GROUP)

    for u in range(n):
        y_send[u] = y_tiles[u].astype(BF16)
    for r in range(1, n):
        exchange(y_send, y_recv, y_ssem, y_rsem, r).start()
    y_recv[me] = y_send[me]

    for r in range(1, n):
        exchange(d_send, d_recv, d_ssem, d_rsem, r).wait_recv()
    def put(group, result):
        folded = gather_own(result)
        for s in range(n):
            fgrad_ref[0, rows_at(group * GROUP, GROUP), s * BLOCK : (s + 1) * BLOCK] = folded[s * GROUP : (s + 1) * GROUP]

    def both_tiles(two):
        return [d_recv[v, rows_at(two * 16, 16), :].astype(F32) for v in range(n)]

    half = slice(0, 256)
    fill(left_even, 0, advance([x[:GROUP] for x in both_tiles(0)]))

    @pl.loop(0, BLOCK // GROUP // 2)
    def _(two):
        group = two * 2
        result = correlate(left_even[half], group)
        fill(left_odd, 0, advance([x[GROUP:] for x in both_tiles(two)]))
        put(group, result)
        result = correlate(left_odd[half], group + 1)
        fill(left_even, 0, advance([x[:GROUP] for x in both_tiles(jnp.minimum(two + 1, last // 2))]))
        put(group + 1, result)

    for r in range(1, n):
        exchange(y_send, y_recv, y_ssem, y_rsem, r).wait_recv()

    @pl.loop(0, n)
    def _(p):
        here = rows_at(p * BLOCK, BLOCK)
        y = jnp.dot(y_recv[p], flip, preferred_element_type=F32)
        out_ref[:, here] = (q_t[here, :] * y).T.astype(BF16)

    @pl.when(me < n - 1)
    def _():
        for copy in halo_copies:
            copy.wait_send()

    for copy in own_sends:
        copy.wait_send()

    @pl.when(middle)
    def _():
        for chunk in range(CHUNKS):
            for which, block in enumerate((near, far)):
                forward_copy(which, block, chunk).wait_send()

    for r in range(1, n):
        exchange(g_send, g_recv, g_ssem, g_rsem, r).wait_send()
        exchange(y_send, y_recv, y_ssem, y_rsem, r).wait_send()
        exchange(d_send, d_recv, d_ssem, d_rsem, r).wait_send()


def on_device(q_in, k_in, v_in, short_filters, long_filter, out_weight, out_grad):
    tokens, group_w = q_in.shape
    taps = short_filters.shape[1]
    channels, length = long_filter.shape[1:]
    n, chans = lax.axis_size("seq"), lax.axis_size("chan")
    fits = (tokens, channels, n, chans, taps, length) == (BLOCK, BLOCK, 8, 4, 3, 8 * BLOCK)
    if not fits or out_weight.shape != (n * BLOCK, chans * group_w):
        return on_device_by_spectrum(q_in, k_in, v_in, short_filters, long_filter, out_weight, out_grad)
    dma = pltpu.SemaphoreType.DMA
    blocks = (n, BLOCK, BLOCK)
    return pl.pallas_call(
        kernel,
        out_shape=(
            jax.ShapeDtypeStruct(q_in.shape, BF16),
            jax.ShapeDtypeStruct(long_filter.shape, F32),
        ),
        in_specs=[pl.BlockSpec(memory_space=pl.ANY)] * 7,
        out_specs=[pl.BlockSpec(memory_space=pltpu.VMEM)] * 2,
        scratch_shapes=[
            pltpu.VMEM((3, tokens, group_w), BF16),
            pltpu.VMEM((3, 16, group_w), BF16),
            pltpu.VMEM(short_filters.shape, F32),
            pltpu.VMEM(blocks, F32),
            pltpu.VMEM(out_weight.shape, BF16),
            pltpu.VMEM((chans, tokens, group_w), BF16),
            pltpu.VMEM((group_w, tokens), F32),
            pltpu.VMEM(blocks, BF16),
            pltpu.VMEM(blocks, BF16),
            pltpu.VMEM(blocks, F32),
            pltpu.VMEM((channels // GROUP, 32 * GROUP, length), BF16),
            pltpu.VMEM(blocks, F32),
            pltpu.VMEM(blocks, F32),
            pltpu.VMEM(blocks, BF16),
            pltpu.VMEM(blocks, BF16),
            pltpu.VMEM((group_w, tokens), F32),
            pltpu.VMEM(blocks, BF16),
            pltpu.VMEM(blocks, BF16),
            pltpu.VMEM((4 * 32 * GROUP, BLOCK), BF16),
            pltpu.VMEM((64 * GROUP, length), BF16),
            pltpu.VMEM((64 * GROUP, length), BF16),
            dma((6 + n,)),
            dma((3,)),
            dma((3,)),
            dma((2, CHUNKS)),
            dma((chans, CHUNKS)),
            dma((2, CHUNKS)),
            dma((n,)),
            dma((n,)),
            dma((n,)),
            dma((n,)),
            dma((n,)),
            dma((n,)),
        ],
        compiler_params=pltpu.CompilerParams(
            collective_id=0, has_side_effects=True, vmem_limit_bytes=60 * 1024 * 1024
        ),
    )(q_in, k_in, v_in, short_filters, long_filter, out_weight, out_grad)


def solution(mesh):
    in_specs = (
        P("seq", "chan"),
        P("seq", "chan"),
        P("seq", "chan"),
        P(None, None, "chan"),
        P("chan", "seq", None),
        P("chan", None),
        P("seq", "chan"),
    )
    out_specs = (P("seq", "chan"), P("chan", "seq", None))
    return jax.shard_map(
        on_device, mesh=mesh, in_specs=in_specs, out_specs=out_specs, check_vma=False
    )
```

```python
import functools
import math

import jax
import jax.numpy as jnp
from jax import lax
from jax.experimental import pallas as pl
from jax.experimental.pallas import tpu as pltpu
from jax.sharding import PartitionSpec as P

HIGHEST = lax.Precision.HIGHEST


def shifted(value, axis, steps):
    count = lax.axis_size(axis)
    leading, last = (max(0, -steps), min(count, count - steps))
    return lax.ppermute(value, axis, [(source, source + steps) for source in range(leading, last)])


def angle_table(rows, cols, modulus):
    first = jnp.arange(rows, dtype=jnp.int32)[:, None]
    second = jnp.arange(cols, dtype=jnp.int32)[None, :]
    phase = (first * second % modulus).astype(jnp.float32) * (2.0 * math.pi / modulus)
    return (jnp.cos(phase), jnp.sin(phase))


def spectrum(signal, rows_p, cols_q):
    cos_p, sin_p = angle_table(rows_p // 2, rows_p, rows_p)
    first_re = jnp.einsum("cnq,nk->ckq", signal, cos_p, precision=HIGHEST)
    first_im = -jnp.einsum("cnq,nk->ckq", signal, sin_p, precision=HIGHEST)
    cos_t, sin_t = angle_table(rows_p, cols_q, rows_p * cols_q)
    turn_re = first_re * cos_t + first_im * sin_t
    turn_im = first_im * cos_t - first_re * sin_t
    cos_q, sin_q = angle_table(cols_q, cols_q, cols_q)
    out_re = jnp.einsum("ckq,qm->ckm", turn_re, cos_q, precision=HIGHEST) + jnp.einsum(
        "ckq,qm->ckm", turn_im, sin_q, precision=HIGHEST
    )
    out_im = jnp.einsum("ckq,qm->ckm", turn_im, cos_q, precision=HIGHEST) - jnp.einsum(
        "ckq,qm->ckm", turn_re, sin_q, precision=HIGHEST
    )
    return (out_re, out_im)


def signal_back(spec_re, spec_im, rows_p, cols_q):
    cos_q, sin_q = angle_table(cols_q, cols_q, cols_q)
    mid_re = jnp.einsum("ckm,mq->ckq", spec_re, cos_q, precision=HIGHEST) - jnp.einsum(
        "ckm,mq->ckq", spec_im, sin_q, precision=HIGHEST
    )
    mid_im = jnp.einsum("ckm,mq->ckq", spec_re, sin_q, precision=HIGHEST) + jnp.einsum(
        "ckm,mq->ckq", spec_im, cos_q, precision=HIGHEST
    )
    cos_t, sin_t = angle_table(rows_p, cols_q, rows_p * cols_q)
    turn_re = mid_re * cos_t - mid_im * sin_t
    turn_im = mid_re * sin_t + mid_im * cos_t
    cos_p, sin_p = angle_table(rows_p, rows_p // 2, rows_p)
    real_part = jnp.einsum("ckq,kn->cnq", turn_re, cos_p, precision=HIGHEST) - jnp.einsum(
        "ckq,kn->cnq", turn_im, sin_p, precision=HIGHEST
    )
    return real_part / (rows_p * cols_q)


def regroup(blocked):
    return lax.all_to_all(blocked, "seq", split_axis=0, concat_axis=1, tiled=True)


def on_device_by_spectrum(q_in, k_in, v_in, short_filters, long_filter, out_weight, out_grad):
    tokens, group_w = q_in.shape
    taps = short_filters.shape[1]
    streams = jnp.stack((q_in, k_in, v_in))
    before = shifted(streams[:, tokens - (taps - 1) :, :], "seq", 1)
    extended = jnp.concatenate((before, streams), axis=1).astype(jnp.float32)
    conv = short_filters[:, 0, None, :] * extended[:, taps - 1 : taps - 1 + tokens, :]
    for lag in range(1, taps):
        conv = (
            conv
            + short_filters[:, lag, None, :]
            * extended[:, taps - 1 - lag : taps - 1 - lag + tokens, :]
        )
    q_conv = conv[0]
    gated_t = (conv[1] * conv[2]).astype(jnp.bfloat16).T
    channels = long_filter.shape[1]
    length = long_filter.shape[2]
    cols_q = length // tokens
    rows_p = 2 * tokens
    filters = long_filter.reshape(channels, tokens, cols_q)
    z_chan = regroup(gated_t)
    z_re, z_im = spectrum(
        z_chan.astype(jnp.float32).reshape(channels, tokens, cols_q), rows_p, cols_q
    )
    h_re, h_im = spectrum(filters, rows_p, cols_q)
    y_chan = signal_back(z_re * h_re - z_im * h_im, z_re * h_im + z_im * h_re, rows_p, cols_q)
    y_chan = y_chan.reshape(channels, length).astype(jnp.bfloat16)
    y_tok = lax.all_to_all(y_chan, "seq", split_axis=1, concat_axis=0, tiled=True)
    operator_out = (q_conv * y_tok.T.astype(jnp.float32)).astype(jnp.bfloat16)
    grad_gate = jnp.einsum(
        "tw,iw->ti",
        lax.all_gather(out_grad, "chan", axis=1, tiled=True),
        out_weight,
        preferred_element_type=jnp.float32,
    )
    dy_chan = regroup((grad_gate * q_conv).astype(jnp.bfloat16).T)
    d_re, d_im = spectrum(
        dy_chan.astype(jnp.float32).reshape(channels, tokens, cols_q), rows_p, cols_q
    )
    filter_grad = signal_back(z_re * d_re + z_im * d_im, z_re * d_im - z_im * d_re, rows_p, cols_q)
    return (operator_out, filter_grad.reshape(1, channels, length))


MESH = pl.DeviceIdType.MESH
BLOCK = 128
CHUNKS = 4
GROUP = 8
F32 = jnp.float32
BF16 = jnp.bfloat16


def rows_at(start, size):
    return pl.ds(pl.multiple_of(start, size), size)


def kernel(
    q_hbm, k_hbm, v_hbm, taps_hbm, filt_hbm, weight_hbm, grad_hbm,
    out_ref, fgrad_ref,
    streams, halo, taps, filt, weight, grads,
    q_t, g_send, g_recv, g_wide, toep, h_rev, y_tiles, y_send, y_recv,
    acc, d_send, d_recv, left_even, left_odd,
    load_sem, halo_ssem, halo_rsem, gather_ssem, gather_rsem, fwd_ssem,
    g_ssem, g_rsem, y_ssem, y_rsem, d_ssem, d_rsem,
):
    n = g_recv.shape[0]
    me, c = lax.axis_index("seq"), lax.axis_index("chan")
    streams_hbm = (q_hbm, k_hbm, v_hbm)
    cols = grads.shape[2] // CHUNKS

    loads = [pltpu.make_async_copy(ref, streams.at[s], load_sem.at[s]) for s, ref in enumerate(streams_hbm)]
    loads.append(pltpu.make_async_copy(taps_hbm, taps, load_sem.at[3]))
    own_grad = pltpu.make_async_copy(grad_hbm, grads.at[c], load_sem.at[4])
    weight_load = pltpu.make_async_copy(weight_hbm, weight, load_sem.at[5])
    filt_loads = [
        pltpu.make_async_copy(filt_hbm.at[0, :, pl.ds(a * BLOCK, BLOCK)], filt.at[a], load_sem.at[6 + a])
        for a in range(n)
    ]
    for copy in (*loads, own_grad, *filt_loads, weight_load):
        copy.start()

    barrier = pltpu.get_barrier_semaphore()
    for r in range(1, n):
        pl.semaphore_signal(barrier, inc=1, device_id=(lax.rem(me + r, n), c), device_id_type=MESH)
    for r in range(1, 4):
        pl.semaphore_signal(barrier, inc=1, device_id=(me, lax.rem(c + r, 4)), device_id_type=MESH)
    pl.semaphore_wait(barrier, n - 1 + 3)

    nxt = lax.rem(me + 1, n)
    halo_copies = [
        pltpu.make_async_remote_copy(
            src_ref=ref.at[pl.ds(BLOCK - 16, 16), :], dst_ref=halo.at[s],
            send_sem=halo_ssem.at[s], recv_sem=halo_rsem.at[s],
            device_id=(nxt, c), device_id_type=MESH,
        )
        for s, ref in enumerate(streams_hbm)
    ]

    @pl.when(me < n - 1)
    def _():
        for copy in halo_copies:
            copy.start()

    @pl.when(me == 0)
    def _():
        halo[...] = jnp.zeros_like(halo)

    partner = c + 1 - 2 * lax.rem(c, 2)
    half = c // 2
    near = 2 - half
    far = 3 - 3 * half
    middle = jnp.logical_or(c == 1, c == 2)

    def gather_copy(block, chunk, src, dst_chan, ssem):
        return pltpu.make_async_remote_copy(
            src_ref=src, dst_ref=grads.at[block, :, pl.ds(chunk * cols, cols)],
            send_sem=ssem, recv_sem=gather_rsem.at[block, chunk],
            device_id=(me, dst_chan), device_id_type=MESH,
        )

    own_sends = []
    for chunk in range(CHUNKS):
        src = grad_hbm.at[:, pl.ds(chunk * cols, cols)]
        own_sends.append(gather_copy(c, chunk, src, partner, gather_ssem.at[0, chunk]))
        own_sends.append(gather_copy(c, chunk, src, near, gather_ssem.at[1, chunk]))
    for copy in own_sends:
        copy.start()

    def forward_copy(which, block, chunk):
        src = grads.at[block, :, pl.ds(chunk * cols, cols)]
        return gather_copy(block, chunk, src, partner, fwd_ssem.at[which, chunk])

    def forward(chunk):
        @pl.when(middle)
        def _():
            for which, block in enumerate((near, far)):
                copy = forward_copy(which, block, chunk)
                copy.wait_recv()
                copy.start()

    row = lax.broadcasted_iota(jnp.int32, (BLOCK, BLOCK), 0)
    lane = lax.broadcasted_iota(jnp.int32, (BLOCK, BLOCK), 1)
    flip = jnp.where(row + lane == BLOCK - 1, 1.0, 0.0).astype(BF16)

    def advance(tiles):
        pairs = []
        lane8 = lane[:8]
        for r in range(4):
            turned = [pltpu.roll(x, BLOCK - 32 * r, 1) if r else x for x in tiles]
            if r:
                after = turned[1:] + [jnp.zeros_like(turned[0])]
                turned = [jnp.where(lane8 < BLOCK - 32 * r, x, y) for x, y in zip(turned, after)]
            turned.append(jnp.zeros_like(turned[0]))
            pairs.append([jnp.concatenate(turned[v : v + 2], axis=0) for v in range(n)])
        return pairs

    def fill(left, first_row, pairs):
        for r in range(4):
            for v in range(n):
                value = pairs[r][v].astype(BF16)
                for m in range(v // 2 + 1):
                    at = first_row + (m * 4 + r) * 16
                    left[at : at + 16, (v - 2 * m) * BLOCK : (v - 2 * m + 1) * BLOCK] = value

    left_even[...] = jnp.zeros_like(left_even)
    left_odd[...] = jnp.zeros_like(left_odd)

    for a in range(n):
        filt_loads[a].wait()
        value = filt[a]
        high = value.astype(BF16)
        low = (value - high.astype(F32)).astype(BF16)
        turned = jnp.dot(high, flip, preferred_element_type=F32) + jnp.dot(low, flip, preferred_element_type=F32)
        h_rev[n - 1 - a] = turned

    for copy in loads:
        copy.wait()

    @pl.when(me > 0)
    def _():
        for copy in halo_copies:
            copy.wait_recv()

    def exchange(send_ref, recv_ref, ssem, rsem, r):
        return pltpu.make_async_remote_copy(
            src_ref=send_ref.at[lax.rem(me + r, n)], dst_ref=recv_ref.at[me],
            send_sem=ssem.at[r], recv_sem=rsem.at[r],
            device_id=(lax.rem(me + r, n), c), device_id_type=MESH,
        )

    for r in range(1, n + 1):
        p = lax.rem(me + r, n)
        here = rows_at(p * BLOCK, BLOCK)
        conv = []
        for s in range(3):
            value = streams[s, :, here].astype(F32)
            tail = halo[s, :, here].astype(F32)
            total = taps[s, 0:1, here] * value
            one = jnp.where(row == 0, tail[15:16, :], pltpu.roll(value, 1, 0))
            total = total + taps[s, 1:2, here] * one
            two = pltpu.roll(value, 2, 0)
            two = jnp.where(row == 0, tail[14:15, :], jnp.where(row == 1, tail[15:16, :], two))
            conv.append(total + taps[s, 2:3, here] * two)
        q_t[here, :] = conv[0].T
        gated = (conv[1] * conv[2]).T.astype(BF16)
        if r < n:
            g_send[p] = gated
            exchange(g_send, g_recv, g_ssem, g_rsem, r).start()
        else:
            g_recv[me] = gated

    lane16 = lax.broadcasted_iota(jnp.int32, (16, BLOCK), 1)
    row16 = lax.broadcasted_iota(jnp.int32, (16, BLOCK), 0)
    keep = [lane16 >= row16 + 16 * k for k in range(2)]

    def build(group):
        for j in range(GROUP):
            other = [jnp.zeros((16, BLOCK), BF16)] * 2
            for u in range(n):
                source = jnp.broadcast_to(g_wide[u, pl.ds(group * GROUP + j, 1), :], (16, BLOCK))
                first = pltpu.roll(source, 0, 1, stride=1, stride_axis=0).astype(BF16)
                turned = [first, pltpu.roll(first, 16, 1)]
                for k in range(2):
                    at = 32 * j + 16 * k
                    toep[group, at : at + 16, u * BLOCK : (u + 1) * BLOCK] = jnp.where(keep[k], turned[k], other[k])
                other = turned

    def correlate(left, group):
        return lax.dot_general(left, toep[group], (((1,), (1,)), ((), ())), preferred_element_type=F32)

    low_half = row[:n] < 4
    place = row[:n] % 4
    strip = lane[:n] // 32

    def gather_own(result):
        tiles = []
        for s in range(n):
            pieces = []
            for r in range(4):
                at = ((s // 2 * 4 + r) * 2 + s % 2) * GROUP
                pieces.append(jnp.where(low_half, result[at : at + GROUP, :BLOCK], result[at : at + GROUP, BLOCK:]))
            tile = None
            for q in range(4):
                mixed = pieces[3]
                for r in range(3):
                    mixed = jnp.where(place == (r - q) % 4, pieces[r], mixed)
                mixed = pltpu.roll(mixed, 32 * q, 1) if q else mixed
                tile = jnp.where(strip == (place + q) % 4, mixed, tile) if q else mixed
            tiles.append(tile)
        return tiles

    def fill_filter(left, group):
        pairs = advance([h_rev[v, rows_at(group * GROUP, GROUP), :] for v in range(n)])
        fill(left, 0, pairs)
        fill(left, 256, [[x - x.astype(BF16).astype(F32) for x in row_of] for row_of in pairs])

    def convolve(left, group):
        result = correlate(left[...], group)
        folded = gather_own(result[:256] + result[256:])
        for s in range(n):
            y_tiles[n - 1 - s, rows_at(group * GROUP, GROUP), :] = folded[s]

    last = BLOCK // GROUP - 1

    def groups(first, end):
        @pl.loop(first // 2, end // 2)
        def _(two):
            group = two * 2
            convolve(left_even, group)
            fill_filter(left_odd, group + 1)
            build(group + 1)
            convolve(left_odd, group + 1)
            fill_filter(left_even, jnp.minimum(group + 2, last))
            build(jnp.minimum(group + 2, last))

    half_cols = 2 * cols

    def add_half(block, half, start):
        at = rows_at(half * half_cols, half_cols)
        size = acc.shape[0] // 2

        @pl.loop(0, 2)
        def _(part):
            here = rows_at(part * size, size)
            term = lax.dot_general(
                weight[here, rows_at(block * grads.shape[2] + half * half_cols, half_cols)], grads[block, :, at],
                (((1,), (1,)), ((), ())), preferred_element_type=F32,
            )
            acc[here, :] = term if start else acc[here, :] + term

    def arrived(block, half):
        for chunk in (2 * half, 2 * half + 1):
            src = grad_hbm.at[:, pl.ds(chunk * cols, cols)]
            gather_copy(block, chunk, src, partner, gather_ssem.at[0, chunk]).wait_recv()

    def others_arrived(half):
        @pl.when(jnp.logical_not(middle))
        def _():
            arrived(near, half)
            arrived(far, half)

        add_half(near, half, False)
        add_half(far, half, False)

    weight_load.wait()
    own_grad.wait()
    add_half(c, 0, True)
    add_half(c, 1, False)
    forward(0)
    fill_filter(left_even, 0)
    forward(1)
    for r in range(1, n):
        exchange(g_send, g_recv, g_ssem, g_rsem, r).wait_recv()
    g_wide[...] = g_recv[...].astype(F32)

    build(0)
    forward(2)
    groups(0, 4)
    forward(3)
    for half in range(2):
        arrived(partner, half)
        add_half(partner, half, False)
    groups(4, 8)
    others_arrived(0)
    groups(8, 10)
    others_arrived(1)
    for r in range(1, n + 1):
        p = lax.rem(me + r, n)
        here = rows_at(p * BLOCK, BLOCK)
        value = (acc[here, :] * q_t[here, :]).astype(BF16)
        if r < n:
            d_send[p] = value
            exchange(d_send, d_recv, d_ssem, d_rsem, r).start()
        else:
            d_recv[me] = value
    groups(10, BLOCK // GROUP)

    for u in range(n):
        y_send[u] = y_tiles[u].astype(BF16)
    for r in range(1, n):
        exchange(y_send, y_recv, y_ssem, y_rsem, r).start()
    y_recv[me] = y_send[me]

    for r in range(1, n):
        exchange(d_send, d_recv, d_ssem, d_rsem, r).wait_recv()
    def put(group, result):
        folded = gather_own(result)
        for s in range(n):
            fgrad_ref[0, rows_at(group * GROUP, GROUP), s * BLOCK : (s + 1) * BLOCK] = folded[s]

    def both_tiles(two):
        return [d_recv[v, rows_at(two * 16, 16), :].astype(F32) for v in range(n)]

    half = slice(0, 256)
    fill(left_even, 0, advance([x[:GROUP] for x in both_tiles(0)]))

    @pl.loop(0, BLOCK // GROUP // 2)
    def _(two):
        group = two * 2
        result = correlate(left_even[half], group)
        fill(left_odd, 0, advance([x[GROUP:] for x in both_tiles(two)]))
        put(group, result)
        result = correlate(left_odd[half], group + 1)
        fill(left_even, 0, advance([x[:GROUP] for x in both_tiles(jnp.minimum(two + 1, last // 2))]))
        put(group + 1, result)

    for r in range(1, n):
        exchange(y_send, y_recv, y_ssem, y_rsem, r).wait_recv()

    @pl.loop(0, n)
    def _(p):
        here = rows_at(p * BLOCK, BLOCK)
        y = jnp.dot(y_recv[p], flip, preferred_element_type=F32)
        out_ref[:, here] = (q_t[here, :] * y).T.astype(BF16)

    @pl.when(me < n - 1)
    def _():
        for copy in halo_copies:
            copy.wait_send()

    for copy in own_sends:
        copy.wait_send()

    @pl.when(middle)
    def _():
        for chunk in range(CHUNKS):
            for which, block in enumerate((near, far)):
                forward_copy(which, block, chunk).wait_send()

    for r in range(1, n):
        exchange(g_send, g_recv, g_ssem, g_rsem, r).wait_send()
        exchange(y_send, y_recv, y_ssem, y_rsem, r).wait_send()
        exchange(d_send, d_recv, d_ssem, d_rsem, r).wait_send()


def on_device(q_in, k_in, v_in, short_filters, long_filter, out_weight, out_grad):
    tokens, group_w = q_in.shape
    taps = short_filters.shape[1]
    channels, length = long_filter.shape[1:]
    n, chans = lax.axis_size("seq"), lax.axis_size("chan")
    fits = (tokens, channels, n, chans, taps, length) == (BLOCK, BLOCK, 8, 4, 3, 8 * BLOCK)
    if not fits or out_weight.shape != (n * BLOCK, chans * group_w):
        return on_device_by_spectrum(q_in, k_in, v_in, short_filters, long_filter, out_weight, out_grad)
    dma = pltpu.SemaphoreType.DMA
    blocks = (n, BLOCK, BLOCK)
    return pl.pallas_call(
        kernel,
        out_shape=(
            jax.ShapeDtypeStruct(q_in.shape, BF16),
            jax.ShapeDtypeStruct(long_filter.shape, F32),
        ),
        in_specs=[pl.BlockSpec(memory_space=pl.ANY)] * 7,
        out_specs=[pl.BlockSpec(memory_space=pltpu.VMEM)] * 2,
        scratch_shapes=[
            pltpu.VMEM((3, tokens, group_w), BF16),
            pltpu.VMEM((3, 16, group_w), BF16),
            pltpu.VMEM(short_filters.shape, F32),
            pltpu.VMEM(blocks, F32),
            pltpu.VMEM(out_weight.shape, BF16),
            pltpu.VMEM((chans, tokens, group_w), BF16),
            pltpu.VMEM((group_w, tokens), F32),
            pltpu.VMEM(blocks, BF16),
            pltpu.VMEM(blocks, BF16),
            pltpu.VMEM(blocks, F32),
            pltpu.VMEM((channels // GROUP, 32 * GROUP, length), BF16),
            pltpu.VMEM(blocks, F32),
            pltpu.VMEM(blocks, F32),
            pltpu.VMEM(blocks, BF16),
            pltpu.VMEM(blocks, BF16),
            pltpu.VMEM((group_w, tokens), F32),
            pltpu.VMEM(blocks, BF16),
            pltpu.VMEM(blocks, BF16),
            pltpu.VMEM((64 * GROUP, length), BF16),
            pltpu.VMEM((64 * GROUP, length), BF16),
            dma((6 + n,)),
            dma((3,)),
            dma((3,)),
            dma((2, CHUNKS)),
            dma((chans, CHUNKS)),
            dma((2, CHUNKS)),
            dma((n,)),
            dma((n,)),
            dma((n,)),
            dma((n,)),
            dma((n,)),
            dma((n,)),
        ],
        compiler_params=pltpu.CompilerParams(
            collective_id=0, has_side_effects=True, vmem_limit_bytes=60 * 1024 * 1024
        ),
    )(q_in, k_in, v_in, short_filters, long_filter, out_weight, out_grad)


def solution(mesh):
    in_specs = (
        P("seq", "chan"),
        P("seq", "chan"),
        P("seq", "chan"),
        P(None, None, "chan"),
        P("chan", "seq", None),
        P("chan", None),
        P("seq", "chan"),
    )
    out_specs = (P("seq", "chan"), P("chan", "seq", None))
    return jax.shard_map(
        on_device, mesh=mesh, in_specs=in_specs, out_specs=out_specs, check_vma=False
    )
```

```python
import functools
import math

import jax
import jax.numpy as jnp
from jax import lax
from jax.experimental import pallas as pl
from jax.experimental.pallas import tpu as pltpu
from jax.sharding import PartitionSpec as P

HIGHEST = lax.Precision.HIGHEST


def shifted(value, axis, steps):
    count = lax.axis_size(axis)
    leading, last = (max(0, -steps), min(count, count - steps))
    return lax.ppermute(value, axis, [(source, source + steps) for source in range(leading, last)])


def angle_table(rows, cols, modulus):
    first = jnp.arange(rows, dtype=jnp.int32)[:, None]
    second = jnp.arange(cols, dtype=jnp.int32)[None, :]
    phase = (first * second % modulus).astype(jnp.float32) * (2.0 * math.pi / modulus)
    return (jnp.cos(phase), jnp.sin(phase))


def spectrum(signal, rows_p, cols_q):
    cos_p, sin_p = angle_table(rows_p // 2, rows_p, rows_p)
    first_re = jnp.einsum("cnq,nk->ckq", signal, cos_p, precision=HIGHEST)
    first_im = -jnp.einsum("cnq,nk->ckq", signal, sin_p, precision=HIGHEST)
    cos_t, sin_t = angle_table(rows_p, cols_q, rows_p * cols_q)
    turn_re = first_re * cos_t + first_im * sin_t
    turn_im = first_im * cos_t - first_re * sin_t
    cos_q, sin_q = angle_table(cols_q, cols_q, cols_q)
    out_re = jnp.einsum("ckq,qm->ckm", turn_re, cos_q, precision=HIGHEST) + jnp.einsum(
        "ckq,qm->ckm", turn_im, sin_q, precision=HIGHEST
    )
    out_im = jnp.einsum("ckq,qm->ckm", turn_im, cos_q, precision=HIGHEST) - jnp.einsum(
        "ckq,qm->ckm", turn_re, sin_q, precision=HIGHEST
    )
    return (out_re, out_im)


def signal_back(spec_re, spec_im, rows_p, cols_q):
    cos_q, sin_q = angle_table(cols_q, cols_q, cols_q)
    mid_re = jnp.einsum("ckm,mq->ckq", spec_re, cos_q, precision=HIGHEST) - jnp.einsum(
        "ckm,mq->ckq", spec_im, sin_q, precision=HIGHEST
    )
    mid_im = jnp.einsum("ckm,mq->ckq", spec_re, sin_q, precision=HIGHEST) + jnp.einsum(
        "ckm,mq->ckq", spec_im, cos_q, precision=HIGHEST
    )
    cos_t, sin_t = angle_table(rows_p, cols_q, rows_p * cols_q)
    turn_re = mid_re * cos_t - mid_im * sin_t
    turn_im = mid_re * sin_t + mid_im * cos_t
    cos_p, sin_p = angle_table(rows_p, rows_p // 2, rows_p)
    real_part = jnp.einsum("ckq,kn->cnq", turn_re, cos_p, precision=HIGHEST) - jnp.einsum(
        "ckq,kn->cnq", turn_im, sin_p, precision=HIGHEST
    )
    return real_part / (rows_p * cols_q)


def regroup(blocked):
    return lax.all_to_all(blocked, "seq", split_axis=0, concat_axis=1, tiled=True)


def on_device_by_spectrum(q_in, k_in, v_in, short_filters, long_filter, out_weight, out_grad):
    tokens, group_w = q_in.shape
    taps = short_filters.shape[1]
    streams = jnp.stack((q_in, k_in, v_in))
    before = shifted(streams[:, tokens - (taps - 1) :, :], "seq", 1)
    extended = jnp.concatenate((before, streams), axis=1).astype(jnp.float32)
    conv = short_filters[:, 0, None, :] * extended[:, taps - 1 : taps - 1 + tokens, :]
    for lag in range(1, taps):
        conv = (
            conv
            + short_filters[:, lag, None, :]
            * extended[:, taps - 1 - lag : taps - 1 - lag + tokens, :]
        )
    q_conv = conv[0]
    gated_t = (conv[1] * conv[2]).astype(jnp.bfloat16).T
    channels = long_filter.shape[1]
    length = long_filter.shape[2]
    cols_q = length // tokens
    rows_p = 2 * tokens
    filters = long_filter.reshape(channels, tokens, cols_q)
    z_chan = regroup(gated_t)
    z_re, z_im = spectrum(
        z_chan.astype(jnp.float32).reshape(channels, tokens, cols_q), rows_p, cols_q
    )
    h_re, h_im = spectrum(filters, rows_p, cols_q)
    y_chan = signal_back(z_re * h_re - z_im * h_im, z_re * h_im + z_im * h_re, rows_p, cols_q)
    y_chan = y_chan.reshape(channels, length).astype(jnp.bfloat16)
    y_tok = lax.all_to_all(y_chan, "seq", split_axis=1, concat_axis=0, tiled=True)
    operator_out = (q_conv * y_tok.T.astype(jnp.float32)).astype(jnp.bfloat16)
    grad_gate = jnp.einsum(
        "tw,iw->ti",
        lax.all_gather(out_grad, "chan", axis=1, tiled=True),
        out_weight,
        preferred_element_type=jnp.float32,
    )
    dy_chan = regroup((grad_gate * q_conv).astype(jnp.bfloat16).T)
    d_re, d_im = spectrum(
        dy_chan.astype(jnp.float32).reshape(channels, tokens, cols_q), rows_p, cols_q
    )
    filter_grad = signal_back(z_re * d_re + z_im * d_im, z_re * d_im - z_im * d_re, rows_p, cols_q)
    return (operator_out, filter_grad.reshape(1, channels, length))


MESH = pl.DeviceIdType.MESH
BLOCK = 128
CHUNKS = 4
GROUP = 8
F32 = jnp.float32
BF16 = jnp.bfloat16


def rows_at(start, size):
    return pl.ds(pl.multiple_of(start, size), size)


def kernel(
    q_hbm, k_hbm, v_hbm, taps_hbm, filt_hbm, weight_hbm, grad_hbm,
    out_ref, fgrad_ref,
    streams, halo, taps, filt, weight, grads,
    q_t, g_send, g_recv, g_wide, toep, h_pad, h_left, y_tiles, y_send, y_recv,
    acc, d_send, d_recv, d_pad, d_even, d_odd, f_tiles,
    load_sem, halo_ssem, halo_rsem, gather_ssem, gather_rsem, fwd_ssem,
    g_ssem, g_rsem, y_ssem, y_rsem, d_ssem, d_rsem,
):
    n = g_recv.shape[0]
    me, c = lax.axis_index("seq"), lax.axis_index("chan")
    streams_hbm = (q_hbm, k_hbm, v_hbm)
    cols = grads.shape[2] // CHUNKS

    loads = [pltpu.make_async_copy(ref, streams.at[s], load_sem.at[s]) for s, ref in enumerate(streams_hbm)]
    loads.append(pltpu.make_async_copy(taps_hbm, taps, load_sem.at[3]))
    own_grad = pltpu.make_async_copy(grad_hbm, grads.at[c], load_sem.at[4])
    weight_load = pltpu.make_async_copy(weight_hbm, weight, load_sem.at[5])
    filt_loads = [
        pltpu.make_async_copy(filt_hbm.at[0, :, pl.ds(a * BLOCK, BLOCK)], filt.at[a], load_sem.at[6 + a])
        for a in range(n)
    ]
    for copy in (*loads, own_grad, *filt_loads, weight_load):
        copy.start()

    barrier = pltpu.get_barrier_semaphore()
    for r in range(1, n):
        pl.semaphore_signal(barrier, inc=1, device_id=(lax.rem(me + r, n), c), device_id_type=MESH)
    for r in range(1, 4):
        pl.semaphore_signal(barrier, inc=1, device_id=(me, lax.rem(c + r, 4)), device_id_type=MESH)
    pl.semaphore_wait(barrier, n - 1 + 3)

    nxt = lax.rem(me + 1, n)
    halo_copies = [
        pltpu.make_async_remote_copy(
            src_ref=ref.at[pl.ds(BLOCK - 16, 16), :], dst_ref=halo.at[s],
            send_sem=halo_ssem.at[s], recv_sem=halo_rsem.at[s],
            device_id=(nxt, c), device_id_type=MESH,
        )
        for s, ref in enumerate(streams_hbm)
    ]

    @pl.when(me < n - 1)
    def _():
        for copy in halo_copies:
            copy.start()

    @pl.when(me == 0)
    def _():
        halo[...] = jnp.zeros_like(halo)

    partner = c + 1 - 2 * lax.rem(c, 2)
    half = c // 2
    near = 2 - half
    far = 3 - 3 * half
    middle = jnp.logical_or(c == 1, c == 2)

    def gather_copy(block, chunk, src, dst_chan, ssem):
        return pltpu.make_async_remote_copy(
            src_ref=src, dst_ref=grads.at[block, :, pl.ds(chunk * cols, cols)],
            send_sem=ssem, recv_sem=gather_rsem.at[block, chunk],
            device_id=(me, dst_chan), device_id_type=MESH,
        )

    own_sends = []
    for chunk in range(CHUNKS):
        src = grad_hbm.at[:, pl.ds(chunk * cols, cols)]
        own_sends.append(gather_copy(c, chunk, src, partner, gather_ssem.at[0, chunk]))
        own_sends.append(gather_copy(c, chunk, src, near, gather_ssem.at[1, chunk]))
    for copy in own_sends:
        copy.start()

    def forward_copy(which, block, chunk):
        src = grads.at[block, :, pl.ds(chunk * cols, cols)]
        return gather_copy(block, chunk, src, partner, fwd_ssem.at[which, chunk])

    def forward(chunk):
        @pl.when(middle)
        def _():
            for which, block in enumerate((near, far)):
                copy = forward_copy(which, block, chunk)
                copy.wait_recv()
                copy.start()

    row = lax.broadcasted_iota(jnp.int32, (BLOCK, BLOCK), 0)
    lane = lax.broadcasted_iota(jnp.int32, (BLOCK, BLOCK), 1)
    flip = jnp.where(row + lane == BLOCK - 1, 1.0, 0.0).astype(BF16)

    def lay_out(pad, blocks):
        for r in range(4):
            turned = [pltpu.roll(x, BLOCK - 32 * r, 1) if r else x for x in blocks]
            for a in range(n):
                value = turned[a]
                if r:
                    after = turned[a + 1] if a + 1 < n else jnp.zeros_like(value)
                    value = jnp.where(lane < BLOCK - 32 * r, value, after)
                pad[r, pl.ds(a, BLOCK, stride=2 * n), :] = value

    def left_rows(pad, channel, r, u):
        at = channel * 2 * n
        return jnp.concatenate([pad[r, pl.ds(at + u, n), :], pad[r + 1, pl.ds(at + u, n), :]], axis=0)

    h_pad[...] = jnp.zeros_like(h_pad)
    d_pad[...] = jnp.zeros_like(d_pad)

    for copy in loads:
        copy.wait()

    @pl.when(me > 0)
    def _():
        for copy in halo_copies:
            copy.wait_recv()

    def exchange(send_ref, recv_ref, ssem, rsem, r):
        return pltpu.make_async_remote_copy(
            src_ref=send_ref.at[lax.rem(me + r, n)], dst_ref=recv_ref.at[me],
            send_sem=ssem.at[r], recv_sem=rsem.at[r],
            device_id=(lax.rem(me + r, n), c), device_id_type=MESH,
        )

    for r in range(1, n + 1):
        p = lax.rem(me + r, n)
        here = rows_at(p * BLOCK, BLOCK)
        conv = []
        for s in range(3):
            value = streams[s, :, here].astype(F32)
            tail = halo[s, :, here].astype(F32)
            total = taps[s, 0:1, here] * value
            one = jnp.where(row == 0, tail[15:16, :], pltpu.roll(value, 1, 0))
            total = total + taps[s, 1:2, here] * one
            two = pltpu.roll(value, 2, 0)
            two = jnp.where(row == 0, tail[14:15, :], jnp.where(row == 1, tail[15:16, :], two))
            conv.append(total + taps[s, 2:3, here] * two)
        q_t[here, :] = conv[0].T
        gated = (conv[1] * conv[2]).T.astype(BF16)
        if r < n:
            g_send[p] = gated
            exchange(g_send, g_recv, g_ssem, g_rsem, r).start()
        else:
            g_recv[me] = gated

    blocks = []
    for a in reversed(range(n)):
        filt_loads[a].wait()
        blocks.append(jnp.dot(filt[a].astype(BF16), flip, preferred_element_type=F32))
    lay_out(h_pad, blocks)

    def fill(left, pad, group):
        for j in range(GROUP):
            for r in (0, 2):
                for u in range(n):
                    at = 32 * j + 8 * r
                    value = left_rows(pad, group * GROUP + j, r, u)
                    left[at : at + 16, u * BLOCK : (u + 1) * BLOCK] = value.astype(BF16)

    @pl.loop(0, BLOCK // GROUP)
    def _(group):
        fill(h_left.at[group], h_pad, group)

    def add_block(at, block):
        if at:
            @pl.when(jnp.logical_or(jnp.logical_not(middle), at == 1))
            def _():
                for chunk in range(CHUNKS):
                    gather_copy(block, chunk, grad_hbm.at[:, pl.ds(chunk * cols, cols)], partner, gather_ssem.at[0, chunk]).wait_recv()

        wide = grads.shape[2]

        @pl.loop(0, 2)
        def _(part):
            size = acc.shape[0] // 2
            here = rows_at(part * size, size)
            term = lax.dot_general(
                weight[here, rows_at(block * wide, wide)], grads[block],
                (((1,), (1,)), ((), ())), preferred_element_type=F32,
            )
            acc[here, :] = term if at == 0 else acc[here, :] + term

    forward(0)
    weight_load.wait()
    own_grad.wait()
    add_block(0, c)
    for r in range(1, n):
        exchange(g_send, g_recv, g_ssem, g_rsem, r).wait_recv()
    g_wide[...] = g_recv[...].astype(F32)

    lane16 = lax.broadcasted_iota(jnp.int32, (16, BLOCK), 1)
    row16 = lax.broadcasted_iota(jnp.int32, (16, BLOCK), 0)
    keep = [lane16 >= row16 + 16 * k for k in range(2)]
    strip = lax.broadcasted_iota(jnp.int32, (n, BLOCK), 1) // 32

    def build(group):
        for j in range(GROUP):
            other = [jnp.zeros((16, BLOCK), BF16)] * 2
            for u in range(n):
                source = jnp.broadcast_to(g_wide[u, pl.ds(group * GROUP + j, 1), :], (16, BLOCK))
                first = pltpu.roll(source, 0, 1, stride=1, stride_axis=0).astype(BF16)
                turned = [first, pltpu.roll(first, 16, 1)]
                for k in range(2):
                    at = 32 * j + 16 * k
                    toep[group, at : at + 16, u * BLOCK : (u + 1) * BLOCK] = jnp.where(keep[k], turned[k], other[k])
                other = turned

    def correlate(left, group):
        return lax.dot_general(left, toep[group], (((1,), (1,)), ((), ())), preferred_element_type=F32)

    def put(tiles, group, result):
        for j in range(GROUP):
            half = j // 4 * BLOCK
            tile = None
            for r in range(4):
                piece = result[32 * j + 8 * r : 32 * j + 8 * r + 8, half : half + BLOCK]
                turn = 32 * (r - j % 4) % BLOCK
                piece = pltpu.roll(piece, turn, 1) if turn else piece
                tile = jnp.where(strip == r, piece, tile) if r else piece
            tiles[rows_at(group * GROUP * n + j * n, n), :] = tile

    def convolve(group):
        put(y_tiles, group, correlate(h_left[group], group))

    def groups(first, last):
        @pl.loop(first, last)
        def _(group):
            convolve(group - 1)
            build(group)

    forward(1)
    build(0)
    groups(1, 3)
    forward(2)
    groups(3, 6)
    forward(3)
    add_block(1, partner)
    groups(6, 10)
    add_block(2, near)
    add_block(3, far)
    for r in range(1, n + 1):
        p = lax.rem(me + r, n)
        here = rows_at(p * BLOCK, BLOCK)
        value = (acc[here, :] * q_t[here, :]).astype(BF16)
        if r < n:
            d_send[p] = value
            exchange(d_send, d_recv, d_ssem, d_rsem, r).start()
        else:
            d_recv[me] = value
    groups(10, BLOCK // GROUP)
    convolve(BLOCK // GROUP - 1)

    for u in range(n):
        y_send[u] = y_tiles[pl.ds(n - 1 - u, BLOCK, stride=n), :].astype(BF16)
    for r in range(1, n):
        exchange(y_send, y_recv, y_ssem, y_rsem, r).start()
    y_recv[me] = y_send[me]

    for r in range(1, n):
        exchange(d_send, d_recv, d_ssem, d_rsem, r).wait_recv()
    lay_out(d_pad, [d_recv[u].astype(F32) for u in range(n)])

    last = BLOCK // GROUP - 1
    fill(d_even, d_pad, 0)

    @pl.loop(0, BLOCK // GROUP // 2)
    def _(two):
        group = two * 2
        result = correlate(d_even[...], group)
        fill(d_odd, d_pad, group + 1)
        put(f_tiles, group, result)
        result = correlate(d_odd[...], group + 1)
        fill(d_even, d_pad, jnp.minimum(group + 2, last))
        put(f_tiles, group + 1, result)

    for s in range(n):
        fgrad_ref[0, :, s * BLOCK : (s + 1) * BLOCK] = f_tiles[pl.ds(s, BLOCK, stride=n), :]

    for r in range(1, n):
        exchange(y_send, y_recv, y_ssem, y_rsem, r).wait_recv()

    @pl.loop(0, n)
    def _(p):
        here = rows_at(p * BLOCK, BLOCK)
        y = jnp.dot(y_recv[p], flip, preferred_element_type=F32)
        out_ref[:, here] = (q_t[here, :] * y).T.astype(BF16)

    @pl.when(me < n - 1)
    def _():
        for copy in halo_copies:
            copy.wait_send()

    for copy in own_sends:
        copy.wait_send()

    @pl.when(middle)
    def _():
        for chunk in range(CHUNKS):
            for which, block in enumerate((near, far)):
                forward_copy(which, block, chunk).wait_send()

    for r in range(1, n):
        exchange(g_send, g_recv, g_ssem, g_rsem, r).wait_send()
        exchange(y_send, y_recv, y_ssem, y_rsem, r).wait_send()
        exchange(d_send, d_recv, d_ssem, d_rsem, r).wait_send()


def publish(out_in, fgrad_in, out_ref, fgrad_ref, sem):
    copies = []
    for i in range(4):
        here = pl.ds(i * 32, 32)
        copies.append(pltpu.make_async_copy(fgrad_in.at[:, here], fgrad_ref.at[:, here], sem.at[i]))
        copies.append(pltpu.make_async_copy(out_in.at[here], out_ref.at[here], sem.at[4 + i]))
    for copy in copies:
        copy.start()
    for copy in copies:
        copy.wait()


def on_device(q_in, k_in, v_in, short_filters, long_filter, out_weight, out_grad):
    tokens, group_w = q_in.shape
    taps = short_filters.shape[1]
    channels, length = long_filter.shape[1:]
    n, chans = lax.axis_size("seq"), lax.axis_size("chan")
    fits = (tokens, channels, n, chans, taps, length) == (BLOCK, BLOCK, 8, 4, 3, 8 * BLOCK)
    if not fits or out_weight.shape != (n * BLOCK, chans * group_w):
        return on_device_by_spectrum(q_in, k_in, v_in, short_filters, long_filter, out_weight, out_grad)
    dma = pltpu.SemaphoreType.DMA
    blocks = (n, BLOCK, BLOCK)
    shapes = (jax.ShapeDtypeStruct(q_in.shape, BF16), jax.ShapeDtypeStruct(long_filter.shape, F32))
    results = pl.pallas_call(
        kernel,
        out_shape=shapes,
        in_specs=[pl.BlockSpec(memory_space=pl.ANY)] * 7,
        out_specs=[pl.BlockSpec(memory_space=pltpu.VMEM)] * 2,
        scratch_shapes=[
            pltpu.VMEM((3, tokens, group_w), BF16),
            pltpu.VMEM((3, 16, group_w), BF16),
            pltpu.VMEM(short_filters.shape, F32),
            pltpu.VMEM(blocks, F32),
            pltpu.VMEM(out_weight.shape, BF16),
            pltpu.VMEM((chans, tokens, group_w), BF16),
            pltpu.VMEM((group_w, tokens), F32),
            pltpu.VMEM(blocks, BF16),
            pltpu.VMEM(blocks, BF16),
            pltpu.VMEM(blocks, F32),
            pltpu.VMEM((channels // GROUP, 32 * GROUP, length), BF16),
            pltpu.VMEM((4, channels * 2 * n, BLOCK), F32),
            pltpu.VMEM((channels // GROUP, 32 * GROUP, length), BF16),
            pltpu.VMEM((channels * n, BLOCK), F32),
            pltpu.VMEM(blocks, BF16),
            pltpu.VMEM(blocks, BF16),
            pltpu.VMEM((group_w, tokens), F32),
            pltpu.VMEM(blocks, BF16),
            pltpu.VMEM(blocks, BF16),
            pltpu.VMEM((4, channels * 2 * n, BLOCK), F32),
            pltpu.VMEM((32 * GROUP, length), BF16),
            pltpu.VMEM((32 * GROUP, length), BF16),
            pltpu.VMEM((channels * n, BLOCK), F32),
            dma((6 + n,)),
            dma((3,)),
            dma((3,)),
            dma((2, CHUNKS)),
            dma((chans, CHUNKS)),
            dma((2, CHUNKS)),
            dma((n,)),
            dma((n,)),
            dma((n,)),
            dma((n,)),
            dma((n,)),
            dma((n,)),
        ],
        compiler_params=pltpu.CompilerParams(
            collective_id=0, has_side_effects=True, vmem_limit_bytes=60 * 1024 * 1024
        ),
    )(q_in, k_in, v_in, short_filters, long_filter, out_weight, out_grad)
    return pl.pallas_call(
        publish,
        out_shape=shapes,
        in_specs=[pl.BlockSpec(memory_space=pl.ANY)] * 2,
        out_specs=[pl.BlockSpec(memory_space=pl.ANY)] * 2,
        scratch_shapes=[dma((8,))],
        compiler_params=pltpu.CompilerParams(vmem_limit_bytes=60 * 1024 * 1024),
    )(*results)


def solution(mesh):
    in_specs = (
        P("seq", "chan"),
        P("seq", "chan"),
        P("seq", "chan"),
        P(None, None, "chan"),
        P("chan", "seq", None),
        P("chan", None),
        P("seq", "chan"),
    )
    out_specs = (P("seq", "chan"), P("chan", "seq", None))
    return jax.shard_map(
        on_device, mesh=mesh, in_specs=in_specs, out_specs=out_specs, check_vma=False
    )
```

```python
import functools
import math

import jax
import jax.numpy as jnp
from jax import lax
from jax.experimental import pallas as pl
from jax.experimental.pallas import tpu as pltpu
from jax.sharding import PartitionSpec as P

HIGHEST = lax.Precision.HIGHEST


def shifted(value, axis, steps):
    count = lax.axis_size(axis)
    leading, last = (max(0, -steps), min(count, count - steps))
    return lax.ppermute(value, axis, [(source, source + steps) for source in range(leading, last)])


def angle_table(rows, cols, modulus):
    first = jnp.arange(rows, dtype=jnp.int32)[:, None]
    second = jnp.arange(cols, dtype=jnp.int32)[None, :]
    phase = (first * second % modulus).astype(jnp.float32) * (2.0 * math.pi / modulus)
    return (jnp.cos(phase), jnp.sin(phase))


def spectrum(signal, rows_p, cols_q):
    cos_p, sin_p = angle_table(rows_p // 2, rows_p, rows_p)
    first_re = jnp.einsum("cnq,nk->ckq", signal, cos_p, precision=HIGHEST)
    first_im = -jnp.einsum("cnq,nk->ckq", signal, sin_p, precision=HIGHEST)
    cos_t, sin_t = angle_table(rows_p, cols_q, rows_p * cols_q)
    turn_re = first_re * cos_t + first_im * sin_t
    turn_im = first_im * cos_t - first_re * sin_t
    cos_q, sin_q = angle_table(cols_q, cols_q, cols_q)
    out_re = jnp.einsum("ckq,qm->ckm", turn_re, cos_q, precision=HIGHEST) + jnp.einsum(
        "ckq,qm->ckm", turn_im, sin_q, precision=HIGHEST
    )
    out_im = jnp.einsum("ckq,qm->ckm", turn_im, cos_q, precision=HIGHEST) - jnp.einsum(
        "ckq,qm->ckm", turn_re, sin_q, precision=HIGHEST
    )
    return (out_re, out_im)


def signal_back(spec_re, spec_im, rows_p, cols_q):
    cos_q, sin_q = angle_table(cols_q, cols_q, cols_q)
    mid_re = jnp.einsum("ckm,mq->ckq", spec_re, cos_q, precision=HIGHEST) - jnp.einsum(
        "ckm,mq->ckq", spec_im, sin_q, precision=HIGHEST
    )
    mid_im = jnp.einsum("ckm,mq->ckq", spec_re, sin_q, precision=HIGHEST) + jnp.einsum(
        "ckm,mq->ckq", spec_im, cos_q, precision=HIGHEST
    )
    cos_t, sin_t = angle_table(rows_p, cols_q, rows_p * cols_q)
    turn_re = mid_re * cos_t - mid_im * sin_t
    turn_im = mid_re * sin_t + mid_im * cos_t
    cos_p, sin_p = angle_table(rows_p, rows_p // 2, rows_p)
    real_part = jnp.einsum("ckq,kn->cnq", turn_re, cos_p, precision=HIGHEST) - jnp.einsum(
        "ckq,kn->cnq", turn_im, sin_p, precision=HIGHEST
    )
    return real_part / (rows_p * cols_q)


def regroup(blocked):
    return lax.all_to_all(blocked, "seq", split_axis=0, concat_axis=1, tiled=True)


def on_device_by_spectrum(q_in, k_in, v_in, short_filters, long_filter, out_weight, out_grad):
    tokens, group_w = q_in.shape
    taps = short_filters.shape[1]
    streams = jnp.stack((q_in, k_in, v_in))
    before = shifted(streams[:, tokens - (taps - 1) :, :], "seq", 1)
    extended = jnp.concatenate((before, streams), axis=1).astype(jnp.float32)
    conv = short_filters[:, 0, None, :] * extended[:, taps - 1 : taps - 1 + tokens, :]
    for lag in range(1, taps):
        conv = (
            conv
            + short_filters[:, lag, None, :]
            * extended[:, taps - 1 - lag : taps - 1 - lag + tokens, :]
        )
    q_conv = conv[0]
    gated_t = (conv[1] * conv[2]).astype(jnp.bfloat16).T
    channels = long_filter.shape[1]
    length = long_filter.shape[2]
    cols_q = length // tokens
    rows_p = 2 * tokens
    filters = long_filter.reshape(channels, tokens, cols_q)
    z_chan = regroup(gated_t)
    z_re, z_im = spectrum(
        z_chan.astype(jnp.float32).reshape(channels, tokens, cols_q), rows_p, cols_q
    )
    h_re, h_im = spectrum(filters, rows_p, cols_q)
    y_chan = signal_back(z_re * h_re - z_im * h_im, z_re * h_im + z_im * h_re, rows_p, cols_q)
    y_chan = y_chan.reshape(channels, length).astype(jnp.bfloat16)
    y_tok = lax.all_to_all(y_chan, "seq", split_axis=1, concat_axis=0, tiled=True)
    operator_out = (q_conv * y_tok.T.astype(jnp.float32)).astype(jnp.bfloat16)
    grad_gate = jnp.einsum(
        "tw,iw->ti",
        lax.all_gather(out_grad, "chan", axis=1, tiled=True),
        out_weight,
        preferred_element_type=jnp.float32,
    )
    dy_chan = regroup((grad_gate * q_conv).astype(jnp.bfloat16).T)
    d_re, d_im = spectrum(
        dy_chan.astype(jnp.float32).reshape(channels, tokens, cols_q), rows_p, cols_q
    )
    filter_grad = signal_back(z_re * d_re + z_im * d_im, z_re * d_im - z_im * d_re, rows_p, cols_q)
    return (operator_out, filter_grad.reshape(1, channels, length))


MESH = pl.DeviceIdType.MESH
BLOCK = 128
CHUNKS = 4
GROUP = 8
F32 = jnp.float32
BF16 = jnp.bfloat16


def rows_at(start, size):
    return pl.ds(pl.multiple_of(start, size), size)


def kernel(
    q_hbm, k_hbm, v_hbm, taps_hbm, filt_hbm, weight_hbm, grad_hbm,
    out_ref, fgrad_ref,
    streams, halo, taps, filt, weight, grads,
    q_t, g_send, g_recv, g_wide, turns, toep, h_pad, h_left, y_tiles, y_send, y_recv,
    acc, d_send, d_recv, d_pad, d_even, d_odd, f_tiles,
    load_sem, halo_ssem, halo_rsem, gather_ssem, gather_rsem, fwd_ssem,
    g_ssem, g_rsem, y_ssem, y_rsem, d_ssem, d_rsem,
):
    n = g_recv.shape[0]
    me, c = lax.axis_index("seq"), lax.axis_index("chan")
    streams_hbm = (q_hbm, k_hbm, v_hbm)
    cols = grads.shape[2] // CHUNKS

    loads = [pltpu.make_async_copy(ref, streams.at[s], load_sem.at[s]) for s, ref in enumerate(streams_hbm)]
    loads.append(pltpu.make_async_copy(taps_hbm, taps, load_sem.at[3]))
    own_grad = pltpu.make_async_copy(grad_hbm, grads.at[c], load_sem.at[4])
    weight_load = pltpu.make_async_copy(weight_hbm, weight, load_sem.at[5])
    filt_loads = [
        pltpu.make_async_copy(filt_hbm.at[0, :, pl.ds(a * BLOCK, BLOCK)], filt.at[a], load_sem.at[6 + a])
        for a in range(n)
    ]
    for copy in (*loads, own_grad, *filt_loads, weight_load):
        copy.start()

    barrier = pltpu.get_barrier_semaphore()
    for r in range(1, n):
        pl.semaphore_signal(barrier, inc=1, device_id=(lax.rem(me + r, n), c), device_id_type=MESH)
    for r in range(1, 4):
        pl.semaphore_signal(barrier, inc=1, device_id=(me, lax.rem(c + r, 4)), device_id_type=MESH)
    pl.semaphore_wait(barrier, n - 1 + 3)

    nxt = lax.rem(me + 1, n)
    halo_copies = [
        pltpu.make_async_remote_copy(
            src_ref=ref.at[pl.ds(BLOCK - 16, 16), :], dst_ref=halo.at[s],
            send_sem=halo_ssem.at[s], recv_sem=halo_rsem.at[s],
            device_id=(nxt, c), device_id_type=MESH,
        )
        for s, ref in enumerate(streams_hbm)
    ]

    @pl.when(me < n - 1)
    def _():
        for copy in halo_copies:
            copy.start()

    @pl.when(me == 0)
    def _():
        halo[...] = jnp.zeros_like(halo)

    partner = c + 1 - 2 * lax.rem(c, 2)
    half = c // 2
    near = 2 - half
    far = 3 - 3 * half
    middle = jnp.logical_or(c == 1, c == 2)

    def gather_copy(block, chunk, src, dst_chan, ssem):
        return pltpu.make_async_remote_copy(
            src_ref=src, dst_ref=grads.at[block, :, pl.ds(chunk * cols, cols)],
            send_sem=ssem, recv_sem=gather_rsem.at[block, chunk],
            device_id=(me, dst_chan), device_id_type=MESH,
        )

    own_sends = []
    for chunk in range(CHUNKS):
        src = grad_hbm.at[:, pl.ds(chunk * cols, cols)]
        own_sends.append(gather_copy(c, chunk, src, partner, gather_ssem.at[0, chunk]))
        own_sends.append(gather_copy(c, chunk, src, near, gather_ssem.at[1, chunk]))
    for copy in own_sends:
        copy.start()

    def forward_copy(which, block, chunk):
        src = grads.at[block, :, pl.ds(chunk * cols, cols)]
        return gather_copy(block, chunk, src, partner, fwd_ssem.at[which, chunk])

    def forward(chunk):
        @pl.when(middle)
        def _():
            for which, block in enumerate((near, far)):
                copy = forward_copy(which, block, chunk)
                copy.wait_recv()
                copy.start()

    row = lax.broadcasted_iota(jnp.int32, (BLOCK, BLOCK), 0)
    lane = lax.broadcasted_iota(jnp.int32, (BLOCK, BLOCK), 1)
    flip = jnp.where(row + lane == BLOCK - 1, 1.0, 0.0).astype(BF16)

    def lay_out(pad, blocks):
        for r in range(4):
            turned = [pltpu.roll(x, BLOCK - 32 * r, 1) if r else x for x in blocks]
            for a in range(n):
                value = turned[a]
                if r:
                    after = turned[a + 1] if a + 1 < n else jnp.zeros_like(value)
                    value = jnp.where(lane < BLOCK - 32 * r, value, after)
                pad[r, pl.ds(a, BLOCK, stride=2 * n), :] = value

    def left_rows(pad, channel, r, u):
        at = channel * 2 * n
        return jnp.concatenate([pad[r, pl.ds(at + u, n), :], pad[r + 1, pl.ds(at + u, n), :]], axis=0)

    h_pad[...] = jnp.zeros_like(h_pad)
    d_pad[...] = jnp.zeros_like(d_pad)

    for copy in loads:
        copy.wait()

    @pl.when(me > 0)
    def _():
        for copy in halo_copies:
            copy.wait_recv()

    def exchange(send_ref, recv_ref, ssem, rsem, r):
        return pltpu.make_async_remote_copy(
            src_ref=send_ref.at[lax.rem(me + r, n)], dst_ref=recv_ref.at[me],
            send_sem=ssem.at[r], recv_sem=rsem.at[r],
            device_id=(lax.rem(me + r, n), c), device_id_type=MESH,
        )

    for r in range(1, n + 1):
        p = lax.rem(me + r, n)
        here = rows_at(p * BLOCK, BLOCK)
        conv = []
        for s in range(3):
            value = streams[s, :, here].astype(F32)
            tail = halo[s, :, here].astype(F32)
            total = taps[s, 0:1, here] * value
            one = jnp.where(row == 0, tail[15:16, :], pltpu.roll(value, 1, 0))
            total = total + taps[s, 1:2, here] * one
            two = pltpu.roll(value, 2, 0)
            two = jnp.where(row == 0, tail[14:15, :], jnp.where(row == 1, tail[15:16, :], two))
            conv.append(total + taps[s, 2:3, here] * two)
        q_t[here, :] = conv[0].T
        gated = (conv[1] * conv[2]).T.astype(BF16)
        if r < n:
            g_send[p] = gated
            exchange(g_send, g_recv, g_ssem, g_rsem, r).start()
        else:
            g_recv[me] = gated

    blocks = []
    for a in reversed(range(n)):
        filt_loads[a].wait()
        blocks.append(jnp.dot(filt[a].astype(BF16), flip, preferred_element_type=F32))
    lay_out(h_pad, blocks)

    def fill(left, pad, group):
        for j in range(GROUP):
            for r in (0, 2):
                for u in range(n):
                    at = 32 * j + 8 * r
                    value = left_rows(pad, group * GROUP + j, r, u)
                    left[at : at + 16, u * BLOCK : (u + 1) * BLOCK] = value.astype(BF16)

    @pl.loop(0, BLOCK // GROUP)
    def _(group):
        fill(h_left.at[group], h_pad, group)

    def add_block(at, block):
        if at:
            @pl.when(jnp.logical_or(jnp.logical_not(middle), at == 1))
            def _():
                for chunk in range(CHUNKS):
                    gather_copy(block, chunk, grad_hbm.at[:, pl.ds(chunk * cols, cols)], partner, gather_ssem.at[0, chunk]).wait_recv()

        wide = grads.shape[2]

        @pl.loop(0, 2)
        def _(part):
            size = acc.shape[0] // 2
            here = rows_at(part * size, size)
            term = lax.dot_general(
                weight[here, rows_at(block * wide, wide)], grads[block],
                (((1,), (1,)), ((), ())), preferred_element_type=F32,
            )
            acc[here, :] = term if at == 0 else acc[here, :] + term

    forward(0)
    weight_load.wait()
    own_grad.wait()
    add_block(0, c)
    for r in range(1, n):
        exchange(g_send, g_recv, g_ssem, g_rsem, r).wait_recv()
    g_wide[...] = g_recv[...].astype(F32)

    lane16 = lax.broadcasted_iota(jnp.int32, (16, BLOCK), 1)
    row16 = lax.broadcasted_iota(jnp.int32, (16, BLOCK), 0)
    keep = [lane16 >= row16 + 16 * k for k in range(2)]
    strip = lax.broadcasted_iota(jnp.int32, (n, BLOCK), 1) // 32

    def build(group):
        for u in range(n):
            value = g_wide[u, rows_at(group * GROUP, GROUP), :]
            for delay in range(16):
                turned = pltpu.roll(value, delay, 1) if delay else value
                turns[pl.ds(u * BLOCK + delay, GROUP, stride=16), :] = turned
        for j in range(GROUP):
            other = [jnp.zeros((16, BLOCK), BF16)] * 2
            for u in range(n):
                first = turns[u * BLOCK + 16 * j : u * BLOCK + 16 * j + 16, :].astype(BF16)
                turned = [first, pltpu.roll(first, 16, 1)]
                for k in range(2):
                    at = 32 * j + 16 * k
                    toep[group, at : at + 16, u * BLOCK : (u + 1) * BLOCK] = jnp.where(keep[k], turned[k], other[k])
                other = turned

    def correlate(left, group):
        return lax.dot_general(left, toep[group], (((1,), (1,)), ((), ())), preferred_element_type=F32)

    def put(tiles, group, result):
        for j in range(GROUP):
            half = j // 4 * BLOCK
            tile = None
            for r in range(4):
                piece = result[32 * j + 8 * r : 32 * j + 8 * r + 8, half : half + BLOCK]
                turn = 32 * (r - j % 4) % BLOCK
                piece = pltpu.roll(piece, turn, 1) if turn else piece
                tile = jnp.where(strip == r, piece, tile) if r else piece
            tiles[rows_at(group * GROUP * n + j * n, n), :] = tile

    def convolve(group):
        put(y_tiles, group, correlate(h_left[group], group))

    def groups(first, last):
        @pl.loop(first, last)
        def _(group):
            convolve(group - 1)
            build(group)

    forward(1)
    build(0)
    groups(1, 3)
    forward(2)
    groups(3, 6)
    forward(3)
    add_block(1, partner)
    groups(6, 10)
    add_block(2, near)
    add_block(3, far)
    for r in range(1, n + 1):
        p = lax.rem(me + r, n)
        here = rows_at(p * BLOCK, BLOCK)
        value = (acc[here, :] * q_t[here, :]).astype(BF16)
        if r < n:
            d_send[p] = value
            exchange(d_send, d_recv, d_ssem, d_rsem, r).start()
        else:
            d_recv[me] = value
    groups(10, BLOCK // GROUP)
    convolve(BLOCK // GROUP - 1)

    for u in range(n):
        y_send[u] = y_tiles[pl.ds(n - 1 - u, BLOCK, stride=n), :].astype(BF16)
    for r in range(1, n):
        exchange(y_send, y_recv, y_ssem, y_rsem, r).start()
    y_recv[me] = y_send[me]

    for r in range(1, n):
        exchange(d_send, d_recv, d_ssem, d_rsem, r).wait_recv()
    lay_out(d_pad, [d_recv[u].astype(F32) for u in range(n)])

    last = BLOCK // GROUP - 1
    fill(d_even, d_pad, 0)

    @pl.loop(0, BLOCK // GROUP // 2)
    def _(two):
        group = two * 2
        result = correlate(d_even[...], group)
        fill(d_odd, d_pad, group + 1)
        put(f_tiles, group, result)
        result = correlate(d_odd[...], group + 1)
        fill(d_even, d_pad, jnp.minimum(group + 2, last))
        put(f_tiles, group + 1, result)

    for s in range(n):
        fgrad_ref[0, :, s * BLOCK : (s + 1) * BLOCK] = f_tiles[pl.ds(s, BLOCK, stride=n), :]

    for r in range(1, n):
        exchange(y_send, y_recv, y_ssem, y_rsem, r).wait_recv()

    @pl.loop(0, n)
    def _(p):
        here = rows_at(p * BLOCK, BLOCK)
        y = jnp.dot(y_recv[p], flip, preferred_element_type=F32)
        out_ref[:, here] = (q_t[here, :] * y).T.astype(BF16)

    @pl.when(me < n - 1)
    def _():
        for copy in halo_copies:
            copy.wait_send()

    for copy in own_sends:
        copy.wait_send()

    @pl.when(middle)
    def _():
        for chunk in range(CHUNKS):
            for which, block in enumerate((near, far)):
                forward_copy(which, block, chunk).wait_send()

    for r in range(1, n):
        exchange(g_send, g_recv, g_ssem, g_rsem, r).wait_send()
        exchange(y_send, y_recv, y_ssem, y_rsem, r).wait_send()
        exchange(d_send, d_recv, d_ssem, d_rsem, r).wait_send()


def publish(out_in, fgrad_in, out_ref, fgrad_ref, out_held, fgrad_held, load_sem, store_sem):
    loads, stores = [], []
    for i in range(4):
        here = pl.ds(i * 32, 32)
        for at, (src, held, dst) in enumerate(
            ((fgrad_in.at[0], fgrad_held, fgrad_ref.at[0]), (out_in, out_held, out_ref))
        ):
            k = 2 * i + at
            loads.append(pltpu.make_async_copy(src.at[here], held.at[here], load_sem.at[k]))
            stores.append(pltpu.make_async_copy(held.at[here], dst.at[here], store_sem.at[k]))
    for copy in loads:
        copy.start()
    for load, store in zip(loads, stores):
        load.wait()
        store.start()
    for copy in stores:
        copy.wait()


def on_device(q_in, k_in, v_in, short_filters, long_filter, out_weight, out_grad):
    tokens, group_w = q_in.shape
    taps = short_filters.shape[1]
    channels, length = long_filter.shape[1:]
    n, chans = lax.axis_size("seq"), lax.axis_size("chan")
    fits = (tokens, channels, n, chans, taps, length) == (BLOCK, BLOCK, 8, 4, 3, 8 * BLOCK)
    if not fits or out_weight.shape != (n * BLOCK, chans * group_w):
        return on_device_by_spectrum(q_in, k_in, v_in, short_filters, long_filter, out_weight, out_grad)
    dma = pltpu.SemaphoreType.DMA
    blocks = (n, BLOCK, BLOCK)
    shapes = (jax.ShapeDtypeStruct(q_in.shape, BF16), jax.ShapeDtypeStruct(long_filter.shape, F32))
    results = pl.pallas_call(
        kernel,
        out_shape=shapes,
        in_specs=[pl.BlockSpec(memory_space=pl.ANY)] * 7,
        out_specs=[pl.BlockSpec(memory_space=pltpu.VMEM)] * 2,
        scratch_shapes=[
            pltpu.VMEM((3, tokens, group_w), BF16),
            pltpu.VMEM((3, 16, group_w), BF16),
            pltpu.VMEM(short_filters.shape, F32),
            pltpu.VMEM(blocks, F32),
            pltpu.VMEM(out_weight.shape, BF16),
            pltpu.VMEM((chans, tokens, group_w), BF16),
            pltpu.VMEM((group_w, tokens), F32),
            pltpu.VMEM(blocks, BF16),
            pltpu.VMEM(blocks, BF16),
            pltpu.VMEM(blocks, F32),
            pltpu.VMEM((n * BLOCK, BLOCK), F32),
            pltpu.VMEM((channels // GROUP, 32 * GROUP, length), BF16),
            pltpu.VMEM((4, channels * 2 * n, BLOCK), F32),
            pltpu.VMEM((channels // GROUP, 32 * GROUP, length), BF16),
            pltpu.VMEM((channels * n, BLOCK), F32),
            pltpu.VMEM(blocks, BF16),
            pltpu.VMEM(blocks, BF16),
            pltpu.VMEM((group_w, tokens), F32),
            pltpu.VMEM(blocks, BF16),
            pltpu.VMEM(blocks, BF16),
            pltpu.VMEM((4, channels * 2 * n, BLOCK), F32),
            pltpu.VMEM((32 * GROUP, length), BF16),
            pltpu.VMEM((32 * GROUP, length), BF16),
            pltpu.VMEM((channels * n, BLOCK), F32),
            dma((6 + n,)),
            dma((3,)),
            dma((3,)),
            dma((2, CHUNKS)),
            dma((chans, CHUNKS)),
            dma((2, CHUNKS)),
            dma((n,)),
            dma((n,)),
            dma((n,)),
            dma((n,)),
            dma((n,)),
            dma((n,)),
        ],
        compiler_params=pltpu.CompilerParams(
            collective_id=0, has_side_effects=True, vmem_limit_bytes=60 * 1024 * 1024
        ),
    )(q_in, k_in, v_in, short_filters, long_filter, out_weight, out_grad)
    return pl.pallas_call(
        publish,
        out_shape=shapes,
        in_specs=[pl.BlockSpec(memory_space=pl.ANY)] * 2,
        out_specs=[pl.BlockSpec(memory_space=pl.ANY)] * 2,
        scratch_shapes=[
            pltpu.VMEM(q_in.shape, BF16),
            pltpu.VMEM(long_filter.shape[1:], F32),
            dma((8,)),
            dma((8,)),
        ],
        compiler_params=pltpu.CompilerParams(vmem_limit_bytes=60 * 1024 * 1024),
    )(*results)


def solution(mesh):
    in_specs = (
        P("seq", "chan"),
        P("seq", "chan"),
        P("seq", "chan"),
        P(None, None, "chan"),
        P("chan", "seq", None),
        P("chan", None),
        P("seq", "chan"),
    )
    out_specs = (P("seq", "chan"), P("chan", "seq", None))
    return jax.shard_map(
        on_device, mesh=mesh, in_specs=in_specs, out_specs=out_specs, check_vma=False
    )
```

```python
import functools
import math

import jax
import jax.numpy as jnp
from jax import lax
from jax.experimental import pallas as pl
from jax.experimental.pallas import tpu as pltpu
from jax.sharding import PartitionSpec as P

HIGHEST = lax.Precision.HIGHEST


def shifted(value, axis, steps):
    count = lax.axis_size(axis)
    leading, last = (max(0, -steps), min(count, count - steps))
    return lax.ppermute(value, axis, [(source, source + steps) for source in range(leading, last)])


def angle_table(rows, cols, modulus):
    first = jnp.arange(rows, dtype=jnp.int32)[:, None]
    second = jnp.arange(cols, dtype=jnp.int32)[None, :]
    phase = (first * second % modulus).astype(jnp.float32) * (2.0 * math.pi / modulus)
    return (jnp.cos(phase), jnp.sin(phase))


def spectrum(signal, rows_p, cols_q):
    cos_p, sin_p = angle_table(rows_p // 2, rows_p, rows_p)
    first_re = jnp.einsum("cnq,nk->ckq", signal, cos_p, precision=HIGHEST)
    first_im = -jnp.einsum("cnq,nk->ckq", signal, sin_p, precision=HIGHEST)
    cos_t, sin_t = angle_table(rows_p, cols_q, rows_p * cols_q)
    turn_re = first_re * cos_t + first_im * sin_t
    turn_im = first_im * cos_t - first_re * sin_t
    cos_q, sin_q = angle_table(cols_q, cols_q, cols_q)
    out_re = jnp.einsum("ckq,qm->ckm", turn_re, cos_q, precision=HIGHEST) + jnp.einsum(
        "ckq,qm->ckm", turn_im, sin_q, precision=HIGHEST
    )
    out_im = jnp.einsum("ckq,qm->ckm", turn_im, cos_q, precision=HIGHEST) - jnp.einsum(
        "ckq,qm->ckm", turn_re, sin_q, precision=HIGHEST
    )
    return (out_re, out_im)


def signal_back(spec_re, spec_im, rows_p, cols_q):
    cos_q, sin_q = angle_table(cols_q, cols_q, cols_q)
    mid_re = jnp.einsum("ckm,mq->ckq", spec_re, cos_q, precision=HIGHEST) - jnp.einsum(
        "ckm,mq->ckq", spec_im, sin_q, precision=HIGHEST
    )
    mid_im = jnp.einsum("ckm,mq->ckq", spec_re, sin_q, precision=HIGHEST) + jnp.einsum(
        "ckm,mq->ckq", spec_im, cos_q, precision=HIGHEST
    )
    cos_t, sin_t = angle_table(rows_p, cols_q, rows_p * cols_q)
    turn_re = mid_re * cos_t - mid_im * sin_t
    turn_im = mid_re * sin_t + mid_im * cos_t
    cos_p, sin_p = angle_table(rows_p, rows_p // 2, rows_p)
    real_part = jnp.einsum("ckq,kn->cnq", turn_re, cos_p, precision=HIGHEST) - jnp.einsum(
        "ckq,kn->cnq", turn_im, sin_p, precision=HIGHEST
    )
    return real_part / (rows_p * cols_q)


def regroup(blocked):
    return lax.all_to_all(blocked, "seq", split_axis=0, concat_axis=1, tiled=True)


def on_device_by_spectrum(q_in, k_in, v_in, short_filters, long_filter, out_weight, out_grad):
    tokens, group_w = q_in.shape
    taps = short_filters.shape[1]
    streams = jnp.stack((q_in, k_in, v_in))
    before = shifted(streams[:, tokens - (taps - 1) :, :], "seq", 1)
    extended = jnp.concatenate((before, streams), axis=1).astype(jnp.float32)
    conv = short_filters[:, 0, None, :] * extended[:, taps - 1 : taps - 1 + tokens, :]
    for lag in range(1, taps):
        conv = (
            conv
            + short_filters[:, lag, None, :]
            * extended[:, taps - 1 - lag : taps - 1 - lag + tokens, :]
        )
    q_conv = conv[0]
    gated_t = (conv[1] * conv[2]).astype(jnp.bfloat16).T
    channels = long_filter.shape[1]
    length = long_filter.shape[2]
    cols_q = length // tokens
    rows_p = 2 * tokens
    filters = long_filter.reshape(channels, tokens, cols_q)
    z_chan = regroup(gated_t)
    z_re, z_im = spectrum(
        z_chan.astype(jnp.float32).reshape(channels, tokens, cols_q), rows_p, cols_q
    )
    h_re, h_im = spectrum(filters, rows_p, cols_q)
    y_chan = signal_back(z_re * h_re - z_im * h_im, z_re * h_im + z_im * h_re, rows_p, cols_q)
    y_chan = y_chan.reshape(channels, length).astype(jnp.bfloat16)
    y_tok = lax.all_to_all(y_chan, "seq", split_axis=1, concat_axis=0, tiled=True)
    operator_out = (q_conv * y_tok.T.astype(jnp.float32)).astype(jnp.bfloat16)
    grad_gate = jnp.einsum(
        "tw,iw->ti",
        lax.all_gather(out_grad, "chan", axis=1, tiled=True),
        out_weight,
        preferred_element_type=jnp.float32,
    )
    dy_chan = regroup((grad_gate * q_conv).astype(jnp.bfloat16).T)
    d_re, d_im = spectrum(
        dy_chan.astype(jnp.float32).reshape(channels, tokens, cols_q), rows_p, cols_q
    )
    filter_grad = signal_back(z_re * d_re + z_im * d_im, z_re * d_im - z_im * d_re, rows_p, cols_q)
    return (operator_out, filter_grad.reshape(1, channels, length))


MESH = pl.DeviceIdType.MESH
BLOCK = 128
CHUNKS = 4
GROUP = 8
F32 = jnp.float32
BF16 = jnp.bfloat16


def rows_at(start, size):
    return pl.ds(pl.multiple_of(start, size), size)


def kernel(
    q_hbm, k_hbm, v_hbm, taps_hbm, filt_hbm, weight_hbm, grad_hbm,
    out_ref, fgrad_ref,
    streams, halo, taps, filt, weight, grads,
    q_t, g_send, g_recv, g_wide, turns, toep, h_pad, h_left, y_tiles, y_send, y_recv,
    acc, d_send, d_recv, d_pad, d_even, d_odd, f_tiles,
    load_sem, halo_ssem, halo_rsem, gather_ssem, gather_rsem, fwd_ssem,
    g_ssem, g_rsem, y_ssem, y_rsem, d_ssem, d_rsem,
):
    n = g_recv.shape[0]
    me, c = lax.axis_index("seq"), lax.axis_index("chan")
    streams_hbm = (q_hbm, k_hbm, v_hbm)
    cols = grads.shape[2] // CHUNKS

    loads = [pltpu.make_async_copy(ref, streams.at[s], load_sem.at[s]) for s, ref in enumerate(streams_hbm)]
    loads.append(pltpu.make_async_copy(taps_hbm, taps, load_sem.at[3]))
    own_grad = pltpu.make_async_copy(grad_hbm, grads.at[c], load_sem.at[4])
    weight_load = pltpu.make_async_copy(weight_hbm, weight, load_sem.at[5])
    filt_loads = [
        pltpu.make_async_copy(filt_hbm.at[0, :, pl.ds(a * BLOCK, BLOCK)], filt.at[a], load_sem.at[6 + a])
        for a in range(n)
    ]
    for copy in (*loads, own_grad, *filt_loads, weight_load):
        copy.start()

    barrier = pltpu.get_barrier_semaphore()
    for r in range(1, n):
        pl.semaphore_signal(barrier, inc=1, device_id=(lax.rem(me + r, n), c), device_id_type=MESH)
    for r in range(1, 4):
        pl.semaphore_signal(barrier, inc=1, device_id=(me, lax.rem(c + r, 4)), device_id_type=MESH)
    pl.semaphore_wait(barrier, n - 1 + 3)

    nxt = lax.rem(me + 1, n)
    halo_copies = [
        pltpu.make_async_remote_copy(
            src_ref=ref.at[pl.ds(BLOCK - 16, 16), :], dst_ref=halo.at[s],
            send_sem=halo_ssem.at[s], recv_sem=halo_rsem.at[s],
            device_id=(nxt, c), device_id_type=MESH,
        )
        for s, ref in enumerate(streams_hbm)
    ]

    @pl.when(me < n - 1)
    def _():
        for copy in halo_copies:
            copy.start()

    @pl.when(me == 0)
    def _():
        halo[...] = jnp.zeros_like(halo)

    partner = c + 1 - 2 * lax.rem(c, 2)
    half = c // 2
    near = 2 - half
    far = 3 - 3 * half
    middle = jnp.logical_or(c == 1, c == 2)

    def gather_copy(block, chunk, src, dst_chan, ssem):
        return pltpu.make_async_remote_copy(
            src_ref=src, dst_ref=grads.at[block, :, pl.ds(chunk * cols, cols)],
            send_sem=ssem, recv_sem=gather_rsem.at[block, chunk],
            device_id=(me, dst_chan), device_id_type=MESH,
        )

    own_sends = []
    for chunk in range(CHUNKS):
        src = grad_hbm.at[:, pl.ds(chunk * cols, cols)]
        own_sends.append(gather_copy(c, chunk, src, partner, gather_ssem.at[0, chunk]))
        own_sends.append(gather_copy(c, chunk, src, near, gather_ssem.at[1, chunk]))
    for copy in own_sends:
        copy.start()

    def forward_copy(which, block, chunk):
        src = grads.at[block, :, pl.ds(chunk * cols, cols)]
        return gather_copy(block, chunk, src, partner, fwd_ssem.at[which, chunk])

    def forward(chunk):
        @pl.when(middle)
        def _():
            for which, block in enumerate((near, far)):
                copy = forward_copy(which, block, chunk)
                copy.wait_recv()
                copy.start()

    row = lax.broadcasted_iota(jnp.int32, (BLOCK, BLOCK), 0)
    lane = lax.broadcasted_iota(jnp.int32, (BLOCK, BLOCK), 1)
    flip = jnp.where(row + lane == BLOCK - 1, 1.0, 0.0).astype(BF16)

    def lay_out(pad, blocks):
        for r in range(4):
            turned = [pltpu.roll(x, BLOCK - 32 * r, 1) if r else x for x in blocks]
            for a in range(n):
                value = turned[a]
                if r:
                    after = turned[a + 1] if a + 1 < n else jnp.zeros_like(value)
                    value = jnp.where(lane < BLOCK - 32 * r, value, after)
                pad[r, pl.ds(a, BLOCK, stride=2 * n), :] = value

    def left_rows(pad, channel, r, u):
        at = channel * 2 * n
        return jnp.concatenate([pad[r, pl.ds(at + u, n), :], pad[r + 1, pl.ds(at + u, n), :]], axis=0)

    h_pad[...] = jnp.zeros_like(h_pad)
    d_pad[...] = jnp.zeros_like(d_pad)

    for copy in loads:
        copy.wait()

    @pl.when(me > 0)
    def _():
        for copy in halo_copies:
            copy.wait_recv()

    def exchange(send_ref, recv_ref, ssem, rsem, r):
        return pltpu.make_async_remote_copy(
            src_ref=send_ref.at[lax.rem(me + r, n)], dst_ref=recv_ref.at[me],
            send_sem=ssem.at[r], recv_sem=rsem.at[r],
            device_id=(lax.rem(me + r, n), c), device_id_type=MESH,
        )

    for r in range(1, n + 1):
        p = lax.rem(me + r, n)
        here = rows_at(p * BLOCK, BLOCK)
        conv = []
        for s in range(3):
            value = streams[s, :, here].astype(F32)
            tail = halo[s, :, here].astype(F32)
            total = taps[s, 0:1, here] * value
            one = jnp.where(row == 0, tail[15:16, :], pltpu.roll(value, 1, 0))
            total = total + taps[s, 1:2, here] * one
            two = pltpu.roll(value, 2, 0)
            two = jnp.where(row == 0, tail[14:15, :], jnp.where(row == 1, tail[15:16, :], two))
            conv.append(total + taps[s, 2:3, here] * two)
        q_t[here, :] = conv[0].T
        gated = (conv[1] * conv[2]).T.astype(BF16)
        if r < n:
            g_send[p] = gated
            exchange(g_send, g_recv, g_ssem, g_rsem, r).start()
        else:
            g_recv[me] = gated

    blocks = []
    for a in reversed(range(n)):
        filt_loads[a].wait()
        blocks.append(jnp.dot(filt[a].astype(BF16), flip, preferred_element_type=F32))
    lay_out(h_pad, blocks)

    def fill(left, pad, group):
        for j in range(GROUP):
            for r in (0, 2):
                for u in range(n):
                    at = 32 * j + 8 * r
                    value = left_rows(pad, group * GROUP + j, r, u)
                    left[at : at + 16, u * BLOCK : (u + 1) * BLOCK] = value.astype(BF16)

    @pl.loop(0, BLOCK // GROUP)
    def _(group):
        fill(h_left.at[group], h_pad, group)

    def add_block(at, block):
        if at:
            @pl.when(jnp.logical_or(jnp.logical_not(middle), at == 1))
            def _():
                for chunk in range(CHUNKS):
                    gather_copy(block, chunk, grad_hbm.at[:, pl.ds(chunk * cols, cols)], partner, gather_ssem.at[0, chunk]).wait_recv()

        wide = grads.shape[2]

        @pl.loop(0, 2)
        def _(part):
            size = acc.shape[0] // 2
            here = rows_at(part * size, size)
            term = lax.dot_general(
                weight[here, rows_at(block * wide, wide)], grads[block],
                (((1,), (1,)), ((), ())), preferred_element_type=F32,
            )
            acc[here, :] = term if at == 0 else acc[here, :] + term

    forward(0)
    weight_load.wait()
    own_grad.wait()
    add_block(0, c)
    for r in range(1, n):
        exchange(g_send, g_recv, g_ssem, g_rsem, r).wait_recv()
    g_wide[...] = g_recv[...].astype(F32)

    lane16 = lax.broadcasted_iota(jnp.int32, (16, BLOCK), 1)
    row16 = lax.broadcasted_iota(jnp.int32, (16, BLOCK), 0)
    keep = [lane16 >= row16 + 16 * k for k in range(2)]
    strip = lax.broadcasted_iota(jnp.int32, (n, BLOCK), 1) // 32

    def build(group):
        for u in range(n):
            value = g_wide[u, rows_at(group * GROUP, GROUP), :]
            for delay in range(16):
                turned = pltpu.roll(value, delay, 1) if delay else value
                turns[pl.ds(u * BLOCK + delay, GROUP, stride=16), :] = turned
        for j in range(GROUP):
            other = [jnp.zeros((16, BLOCK), BF16)] * 2
            for u in range(n):
                first = turns[u * BLOCK + 16 * j : u * BLOCK + 16 * j + 16, :].astype(BF16)
                turned = [first, pltpu.roll(first, 16, 1)]
                for k in range(2):
                    at = 32 * j + 16 * k
                    toep[group, at : at + 16, u * BLOCK : (u + 1) * BLOCK] = jnp.where(keep[k], turned[k], other[k])
                other = turned

    def correlate(left, group):
        return lax.dot_general(left, toep[group], (((1,), (1,)), ((), ())), preferred_element_type=F32)

    def put(tiles, group, result):
        for j in range(GROUP):
            half = j // 4 * BLOCK
            tile = None
            for r in range(4):
                piece = result[32 * j + 8 * r : 32 * j + 8 * r + 8, half : half + BLOCK]
                turn = 32 * (r - j % 4) % BLOCK
                piece = pltpu.roll(piece, turn, 1) if turn else piece
                tile = jnp.where(strip == r, piece, tile) if r else piece
            tiles[rows_at(group * GROUP * n + j * n, n), :] = tile

    def convolve(group):
        put(y_tiles, group, correlate(h_left[group], group))

    def groups(first, last):
        @pl.loop(first, last)
        def _(group):
            convolve(group - 1)
            build(group)

    forward(1)
    build(0)
    groups(1, 2)
    forward(2)
    groups(2, 4)
    forward(3)
    add_block(1, partner)
    groups(4, 10)
    add_block(2, near)
    add_block(3, far)
    for r in range(1, n + 1):
        p = lax.rem(me + r, n)
        here = rows_at(p * BLOCK, BLOCK)
        value = (acc[here, :] * q_t[here, :]).astype(BF16)
        if r < n:
            d_send[p] = value
            exchange(d_send, d_recv, d_ssem, d_rsem, r).start()
        else:
            d_recv[me] = value
    groups(10, BLOCK // GROUP)
    convolve(BLOCK // GROUP - 1)

    for u in range(n):
        y_send[u] = y_tiles[pl.ds(n - 1 - u, BLOCK, stride=n), :].astype(BF16)
    for r in range(1, n):
        exchange(y_send, y_recv, y_ssem, y_rsem, r).start()
    y_recv[me] = y_send[me]

    for r in range(1, n):
        exchange(d_send, d_recv, d_ssem, d_rsem, r).wait_recv()
    lay_out(d_pad, [d_recv[u].astype(F32) for u in range(n)])

    last = BLOCK // GROUP - 1
    fill(d_even, d_pad, 0)

    @pl.loop(0, BLOCK // GROUP // 2)
    def _(two):
        group = two * 2
        result = correlate(d_even[...], group)
        fill(d_odd, d_pad, group + 1)
        put(f_tiles, group, result)
        result = correlate(d_odd[...], group + 1)
        fill(d_even, d_pad, jnp.minimum(group + 2, last))
        put(f_tiles, group + 1, result)

    for s in range(n):
        fgrad_ref[0, :, s * BLOCK : (s + 1) * BLOCK] = f_tiles[pl.ds(s, BLOCK, stride=n), :]

    for r in range(1, n):
        exchange(y_send, y_recv, y_ssem, y_rsem, r).wait_recv()

    @pl.loop(0, n)
    def _(p):
        here = rows_at(p * BLOCK, BLOCK)
        y = jnp.dot(y_recv[p], flip, preferred_element_type=F32)
        out_ref[:, here] = (q_t[here, :] * y).T.astype(BF16)

    @pl.when(me < n - 1)
    def _():
        for copy in halo_copies:
            copy.wait_send()

    for copy in own_sends:
        copy.wait_send()

    @pl.when(middle)
    def _():
        for chunk in range(CHUNKS):
            for which, block in enumerate((near, far)):
                forward_copy(which, block, chunk).wait_send()

    for r in range(1, n):
        exchange(g_send, g_recv, g_ssem, g_rsem, r).wait_send()
        exchange(y_send, y_recv, y_ssem, y_rsem, r).wait_send()
        exchange(d_send, d_recv, d_ssem, d_rsem, r).wait_send()


def publish(out_in, fgrad_in, out_ref, fgrad_ref, out_held, fgrad_held, load_sem, store_sem):
    loads, stores = [], []
    for i in range(4):
        here = pl.ds(i * 32, 32)
        for at, (src, held, dst) in enumerate(
            ((fgrad_in.at[0], fgrad_held, fgrad_ref.at[0]), (out_in, out_held, out_ref))
        ):
            k = 2 * i + at
            loads.append(pltpu.make_async_copy(src.at[here], held.at[here], load_sem.at[k]))
            stores.append(pltpu.make_async_copy(held.at[here], dst.at[here], store_sem.at[k]))
    for copy in loads:
        copy.start()
    for load, store in zip(loads, stores):
        load.wait()
        store.start()
    for copy in stores:
        copy.wait()


def on_device(q_in, k_in, v_in, short_filters, long_filter, out_weight, out_grad):
    tokens, group_w = q_in.shape
    taps = short_filters.shape[1]
    channels, length = long_filter.shape[1:]
    n, chans = lax.axis_size("seq"), lax.axis_size("chan")
    fits = (tokens, channels, n, chans, taps, length) == (BLOCK, BLOCK, 8, 4, 3, 8 * BLOCK)
    if not fits or out_weight.shape != (n * BLOCK, chans * group_w):
        return on_device_by_spectrum(q_in, k_in, v_in, short_filters, long_filter, out_weight, out_grad)
    dma = pltpu.SemaphoreType.DMA
    blocks = (n, BLOCK, BLOCK)
    shapes = (jax.ShapeDtypeStruct(q_in.shape, BF16), jax.ShapeDtypeStruct(long_filter.shape, F32))
    results = pl.pallas_call(
        kernel,
        out_shape=shapes,
        in_specs=[pl.BlockSpec(memory_space=pl.ANY)] * 7,
        out_specs=[pl.BlockSpec(memory_space=pltpu.VMEM)] * 2,
        scratch_shapes=[
            pltpu.VMEM((3, tokens, group_w), BF16),
            pltpu.VMEM((3, 16, group_w), BF16),
            pltpu.VMEM(short_filters.shape, F32),
            pltpu.VMEM(blocks, F32),
            pltpu.VMEM(out_weight.shape, BF16),
            pltpu.VMEM((chans, tokens, group_w), BF16),
            pltpu.VMEM((group_w, tokens), F32),
            pltpu.VMEM(blocks, BF16),
            pltpu.VMEM(blocks, BF16),
            pltpu.VMEM(blocks, F32),
            pltpu.VMEM((n * BLOCK, BLOCK), F32),
            pltpu.VMEM((channels // GROUP, 32 * GROUP, length), BF16),
            pltpu.VMEM((4, channels * 2 * n, BLOCK), F32),
            pltpu.VMEM((channels // GROUP, 32 * GROUP, length), BF16),
            pltpu.VMEM((channels * n, BLOCK), F32),
            pltpu.VMEM(blocks, BF16),
            pltpu.VMEM(blocks, BF16),
            pltpu.VMEM((group_w, tokens), F32),
            pltpu.VMEM(blocks, BF16),
            pltpu.VMEM(blocks, BF16),
            pltpu.VMEM((4, channels * 2 * n, BLOCK), F32),
            pltpu.VMEM((32 * GROUP, length), BF16),
            pltpu.VMEM((32 * GROUP, length), BF16),
            pltpu.VMEM((channels * n, BLOCK), F32),
            dma((6 + n,)),
            dma((3,)),
            dma((3,)),
            dma((2, CHUNKS)),
            dma((chans, CHUNKS)),
            dma((2, CHUNKS)),
            dma((n,)),
            dma((n,)),
            dma((n,)),
            dma((n,)),
            dma((n,)),
            dma((n,)),
        ],
        compiler_params=pltpu.CompilerParams(
            collective_id=0, has_side_effects=True, vmem_limit_bytes=60 * 1024 * 1024
        ),
    )(q_in, k_in, v_in, short_filters, long_filter, out_weight, out_grad)
    return pl.pallas_call(
        publish,
        out_shape=shapes,
        in_specs=[pl.BlockSpec(memory_space=pl.ANY)] * 2,
        out_specs=[pl.BlockSpec(memory_space=pl.ANY)] * 2,
        scratch_shapes=[
            pltpu.VMEM(q_in.shape, BF16),
            pltpu.VMEM(long_filter.shape[1:], F32),
            dma((8,)),
            dma((8,)),
        ],
        compiler_params=pltpu.CompilerParams(vmem_limit_bytes=60 * 1024 * 1024),
    )(*results)


def solution(mesh):
    in_specs = (
        P("seq", "chan"),
        P("seq", "chan"),
        P("seq", "chan"),
        P(None, None, "chan"),
        P("chan", "seq", None),
        P("chan", None),
        P("seq", "chan"),
    )
    out_specs = (P("seq", "chan"), P("chan", "seq", None))
    return jax.shard_map(
        on_device, mesh=mesh, in_specs=in_specs, out_specs=out_specs, check_vma=False
    )
```
